256 devices in a mesh: lat: 4 (over x), lon: 64 (over z, y, core).
Axes of the slice: x: 4, y: 4, z: 8, core: 2. Of those that a mesh axis runs over, the one named last changes fastest.
Arguments:
- field: float32 [1024, 8640], P('lat', 'lon'), may hold values from -6 to 6
- quad_weight: float32 [1024], P('lat'), may hold values from 0.2 to 1
- legendre: bfloat16 [512, 1025, 1024], P('lon', None, 'lat'), may hold values from -0.75 to 0.75
- love_factor: float32 [1024], replicated, may hold values from 0.1 to 1
- pair_table: int32 [512], P('lon'), may hold values from 0 to 511, each once
Outputs:
- sal_field: float32 [1024, 8640], P('lat', 'lon')
The draws below stay inside these ranges and needn't reach their ends.
Inputs may be any that keep to these rules, and one draw needn't show every extreme that they name: `pair_table`: each pair number stands once; pair p holds the orders p and 1023 - p.
All inputs are finite; a program needn't handle non-finite values.
Results may differ from the reference program's by a relative error of at most 0.0047.
Values may be sent and summed in bfloat16 or wider, within the bound.
A program may use at most 64 MiB of HBM per device.

```python
import math
import jax
import jax.numpy as jnp
from jax import lax

NLON = 8640
NORD = 1024
NLAT = 1024
NPAIRS = 512
NPACK = 1025


def shard_levels(own_key, shape, split, least, top_value):
    def one(axis_at, parts):
        steps = jax.random.uniform(jax.random.fold_in(jax.random.fold_in(own_key, 6), axis_at), (parts,), jnp.float32, least / len(split), top_value / len(split))
        return jnp.repeat(jnp.exp(steps), shape[axis_at] // parts).reshape((-1,) + (1,) * (len(shape) - axis_at - 1))

    factor_of = one(*split[0])
    for cut in split[1:]:
        factor_of = factor_of * one(*cut)
    return factor_of


def gaussian(rng, dims, spread, most, split=(), kind=jnp.bfloat16):
    drawn = spread * jax.random.normal(rng, dims, jnp.float32)
    if split:
        drawn = drawn * shard_levels(rng, dims, split, -0.22, 0.18)
    return jnp.clip(drawn, -most, most).astype(kind)


def setup_inputs(seed: int = 0) -> dict:
    arg_keys = jax.random.split(jax.random.key(seed), 6)
    field = gaussian(arg_keys[0], (NLAT, NLON), 1.0, 6.0, ((0, 4), (1, 64)), jnp.float32)
    quad_weight = jnp.clip(0.2 + 0.8 * jax.random.uniform(arg_keys[1], (NLAT,), jnp.float32) ** shard_levels(arg_keys[1], (NLAT,), ((0, 4),), -0.2, 0.2), 0.2, 1.0)
    legendre = gaussian(arg_keys[2], (NPAIRS, NPACK, NLAT), (NORD // 14) ** -0.5, 0.75, ((0, 64), (2, 4)))
    love_factor = jnp.clip(jnp.exp(jax.random.uniform(arg_keys[3], (NORD,), jnp.float32, math.log(0.1), math.log(1.0))), 0.1, 1.0)
    pair_table = jax.random.permutation(arg_keys[4], NPAIRS).astype(jnp.int32)
    return dict(field=field, quad_weight=quad_weight, legendre=legendre, love_factor=love_factor, pair_table=pair_table)


def reference(field, quad_weight, legendre, love_factor, pair_table):
    spectrum = jnp.fft.rfft(field, axis=1)[:, :NORD]
    real_part = (jnp.real(spectrum) / NLON * quad_weight[:, None]).astype(jnp.bfloat16)
    imag_part = (jnp.imag(spectrum) / NLON * quad_weight[:, None]).astype(jnp.bfloat16)
    real_rows = real_part.T
    imag_rows = imag_part.T
    padded = jnp.concatenate([jnp.zeros((1,), jnp.float32), love_factor, jnp.zeros((NPACK + 1,), jnp.float32)])
    position = jnp.arange(NPACK, dtype=jnp.int32)

    def one_pair(packed_args):
        pair_index, matrix = packed_args
        high_order = NORD - 1 - pair_index
        fourier = jnp.stack([real_rows[pair_index], imag_rows[pair_index], real_rows[high_order], imag_rows[high_order]])
        both_parts = jnp.dot(fourier, matrix.T, preferred_element_type=jnp.float32)
        is_low = position < NORD - pair_index
        coefficient = jnp.where(is_low[None], both_parts[0:2], both_parts[2:4])
        low_love = lax.dynamic_slice_in_dim(padded, (pair_index + 1).astype(jnp.int32), NPACK)
        factor = jnp.where(is_low, low_love, padded[:NPACK])
        spectral = (coefficient * factor).astype(jnp.bfloat16)
        blank_part = jnp.zeros_like(spectral)
        split_parts = jnp.concatenate([jnp.where(is_low[None], spectral, blank_part), jnp.where(is_low[None], blank_part, spectral)])
        return jnp.dot(split_parts, matrix, preferred_element_type=jnp.float32).astype(jnp.bfloat16)

    fields = lax.map(one_pair, (pair_table, legendre))
    values = fields.astype(jnp.float32)
    low_ids = pair_table
    high_ids = (NORD - 1 - pair_table).astype(jnp.int32)
    dense_re = jnp.zeros((NORD, NLAT), jnp.float32).at[low_ids].set(values[:, 0]).at[high_ids].set(values[:, 2])
    dense_im = jnp.zeros((NORD, NLAT), jnp.float32).at[low_ids].set(values[:, 1]).at[high_ids].set(values[:, 3])
    padding_rows = jnp.zeros((NLON // 2 + 1 - NORD, NLAT), jnp.float32)
    spectrum_out = lax.complex(jnp.concatenate([dense_re, padding_rows]), jnp.concatenate([dense_im, padding_rows]))
    grid_out = jnp.fft.irfft(spectrum_out, n=NLON, axis=0) * NLON
    return grid_out.T.astype(jnp.float32)
```

```python
import math

import jax
import jax.numpy as jnp
import ml_dtypes
import numpy as np
from jax import lax
from jax.experimental import pallas as pl
from jax.experimental.pallas import tpu as pltpu
from jax.sharding import PartitionSpec as P

F32 = jnp.float32
BF16 = jnp.bfloat16
TOTAL_LON = 8640
LON_COLS = 135
DEGREES = 1024
GROUPS = ((0, 4), (1, 7), (2, 6), (3, 5))
FAR_FIRST = (4, 3, 5, 2, 6, 1, 7)


def pair_orders():
    steps = 8 * np.arange(64)
    low = np.concatenate([steps + r for group in GROUPS for r in group])
    high = np.concatenate([steps + 7 - r for group in GROUPS for r in group])
    return low, high


def angle_constants():
    low, high = pair_orders()
    columns = np.arange(LON_COLS)
    made = np.zeros((8, 4, 2, 512, 256), ml_dtypes.bfloat16)
    for group in range(4):
        span = slice(128 * group, 128 * group + 128)
        orders = np.concatenate([low[span], DEGREES - 1 - high[span]])
        sign = np.ones((256, 1))
        if group:
            sign[64:128] = -1.0
            sign[192:256] = -1.0
        for q in range(8):
            turns = orders[:, None] * (LON_COLS * q + columns) % TOTAL_LON
            angle = turns * (2.0 * np.pi / TOTAL_LON)
            both = np.concatenate([np.cos(angle), np.sin(angle) * sign])
            head = both.astype(ml_dtypes.bfloat16)
            made[q, group, 0, :, :LON_COLS] = head
            made[q, group, 1, :, :LON_COLS] = (both - head.astype(np.float64)).astype(ml_dtypes.bfloat16)
    return made


def kernel(
    field, quad, love, pairs, perm, legendre, angles, out,
    leg, table, tail, last_rows, s1, r1, rp1, rp2, onehot, rhs, orders_all, s2, r2, s3, r3, four, s4, r4, r5,
    factor, love_rows, blocks, s6, r6, r7, s8, r8,
    local_sem, sem_pz, sem_pq, sem1, sem2, sem3, sem4, sem5, sem6, sem7, sem8,
):
    lon = lax.axis_index("lon")
    x = lax.axis_index("lat")
    z = lon // 8
    q = lon % 8

    def z_device(i):
        return {"lon": i * 8 + q}

    def q_device(i):
        return {"lon": z * 8 + i}

    def x_device(i):
        return {"lat": i}

    barrier = pltpu.get_barrier_semaphore()
    for d in range(1, 8):
        pl.semaphore_signal(barrier, inc=1, device_id=z_device((z + d) % 8))
        pl.semaphore_signal(barrier, inc=1, device_id=q_device((q + d) % 8))
    for d in range(1, 4):
        pl.semaphore_signal(barrier, inc=1, device_id=x_device((x + d) % 4))

    leg_copy = pltpu.make_async_copy(legendre, leg, local_sem.at[0])
    table_copy = pltpu.make_async_copy(angles.at[q], table, local_sem.at[1])
    leg_copy.start()
    table_copy.start()

    started = []

    def send(distances, me, size, device, source, target, sems):
        copies = []
        for d in distances:
            to = (me + d) % size
            copy = pltpu.make_async_remote_copy(
                src_ref=source(to), dst_ref=target(d),
                send_sem=sems.at[0, d], recv_sem=sems.at[1, d],
                device_id=device(to),
            )
            copy.start()
            copies.append(copy)
        started.extend(copies)
        return copies

    def arrive(copies):
        for copy in copies:
            copy.wait_recv()

    lane = lax.broadcasted_iota(jnp.int32, (1, 128), 1)
    quarter = lane // 32
    step_in_tile = lane // 8

    last_rows[...] = jnp.zeros_like(last_rows)
    last_rows[0:15, :] = field[120:135, :]
    for h in range(2):
        cols = slice(128 * h, 128 * h + 128)
        runs = [field[40 * c:40 * c + 40, cols] for c in range(3)] + [last_rows[:, cols]]
        for g in range(4):
            packed = pltpu.roll(runs[0], (32 * (0 - g)) % 128, 1) if g else runs[0]
            for c in range(1, 4):
                moved = pltpu.roll(runs[c], (32 * (c - g)) % 128, 1) if c != g else runs[c]
                packed = jnp.where(quarter == c, moved, packed)
            s1[4 * h + g] = packed

    pl.semaphore_wait(barrier, 17)
    copies_pz = send(FAR_FIRST, z, 8, z_device, lambda to: pairs, lambda d: rp1.at[z], sem_pz)
    copies1 = send(FAR_FIRST, z, 8, z_device, lambda to: s1.at[to], lambda d: r1.at[z], sem1)
    r1[z] = s1[z]
    rp1[z] = pairs[...]

    pair_lane = pairs[0:1, :]
    rhs[...] = jnp.zeros_like(rhs)
    s4[...] = jnp.zeros_like(s4)
    tail[...] = jnp.zeros_like(tail)
    love_rows[...] = jnp.zeros_like(love_rows)
    love_rows[1:9, :] = love[...]
    love16 = love_rows[...]
    lane_row = lax.broadcasted_iota(jnp.int32, (128, 128), 0).astype(F32)
    step_f = step_in_tile.astype(F32)
    tile_row = lax.broadcasted_iota(jnp.int32, (8, 128), 0)

    def shifted_love(start):
        whole = jnp.floor(start * (1.0 / 128.0))
        picked = jnp.where(lane_row == start - 128.0 * whole, 1.0, 0.0).astype(F32)
        rows = jnp.dot(love16, picked, preferred_element_type=F32, precision=lax.Precision.HIGHEST)
        for bit in (4, 2, 1):
            half = jnp.floor(whole * (1.0 / bit))
            odd = half - 2.0 * jnp.floor(half * 0.5)
            rows = jnp.where(odd > 0.5, pltpu.roll(rows, 16 - bit, 0), rows)
        return rows

    def column_ids(t0):
        return 128 * tile_row + (16 * t0 + step_in_tile)

    pair_int = pair_lane.astype(jnp.int32)
    for t0 in range(8):
        low_love = shifted_love(step_f + (pair_lane + (16.0 * t0 + 128.0)))
        high_love = shifted_love(step_f + (16.0 * t0 + 127.0))
        is_low = column_ids(t0) < DEGREES - pair_int
        factor[8 * t0:8 * t0 + 8, :] = jnp.where(is_low, low_love[0:8], high_love[0:8])
        if t0 == 0:
            factor[64:72, :] = high_love[8:16]

    arrive(copies_pz)
    gathered = rp1[0]
    for i in range(1, 8):
        gathered = jnp.where(tile_row == i, rp1[i], gathered)
    mine = pl.ds(pl.multiple_of(8 * q, 8), 8)
    rp2[mine, :] = gathered
    copies_pq = send(FAR_FIRST, q, 8, q_device, lambda to: rp2.at[mine], lambda d: rp2.at[mine], sem_pq)
    arrive(copies_pq)
    wanted = perm[0:1, :]
    diagonal = tile_row == lane

    def onehot_rows(i, carry):
        pieces = []
        for half in range(2):
            row = rp2[pl.ds(2 * i + half, 1), :]
            column = jnp.sum(jnp.where(diagonal, jnp.broadcast_to(row, (8, 128)), 0.0), axis=1, keepdims=True)
            pieces.append(jnp.where(column == wanted, 1.0, 0.0))
        onehot[pl.ds(pl.multiple_of(16 * i, 16), 16), :] = jnp.concatenate(pieces, axis=0).astype(BF16)
        return carry

    lax.fori_loop(0, 32, onehot_rows, 0)

    table_copy.wait()
    arrive(copies1)
    f = [r1[i] for i in range(8)]
    a = [f[i] - f[i + 4] for i in range(4)]
    b = [f[i] + f[i + 4] for i in range(4)]
    root = math.sqrt(0.5)
    a13m = root * (a[1] - a[3])
    a13p = root * (a[1] + a[3])
    parts = (
        (b[0] + b[1] + b[2] + b[3], b[0] - b[1] + b[2] - b[3]),
        (a[0] + a13m, -a[2] - a13p),
        (b[0] - b[2], b[3] - b[1]),
        (a[0] - a13m, a[2] - a13p),
    )

    def turned(value, by):
        return pltpu.roll(value, by % 128, value.ndim - 1) if by % 128 else value

    for g in range(4):
        re, im = parts[g]
        for c in range(4):
            rhs[g, 40 * c:40 * c + 40, :] = jnp.where(
                quarter < 2,
                jnp.where(quarter == 0, turned(re, -32 * c), turned(im, 32 - 32 * c)),
                jnp.where(quarter == 2, turned(re, 64 - 32 * c), turned(im, 96 - 32 * c)),
            )
    for g in range(4):
        value = rhs[g]
        head = value.astype(BF16).astype(F32)
        both = jnp.where(lane < 64, head, value - head).astype(BF16)
        first = jnp.dot(table[g, 0], both, preferred_element_type=F32)
        second = jnp.dot(table[g, 1], both, preferred_element_type=F32)
        total = first + turned(first, 64) + second
        d1, d2 = total[0:256], total[256:512]
        if g:
            spectrum = d1 + jnp.where(quarter == 0, turned(d2, 96), -turned(d2, 32))
            flipped = jnp.where(quarter == 1, -spectrum, spectrum)
            rows = (spectrum[0:64], flipped[64:128], spectrum[128:192], flipped[192:256])
        else:
            plain = jnp.where(quarter == 0, d1, -turned(d2, 32))
            other = jnp.where(quarter == 0, turned(d1, 96), -d2)
            rows = (plain[0:64], other[64:128], plain[128:192], other[192:256])
        for half in range(2):
            at = 128 * g + 64 * half
            orders_all[at:at + 64, :] = jnp.where(lane < 64, rows[half], 0.0)
            orders_all[512 + at:512 + at + 64, :] = jnp.where(lane < 64, 0.0, turned(rows[2 + half], 64))
    value = orders_all[...]
    head = value.astype(BF16)
    rest = (value - head.astype(F32)).astype(BF16)
    in_slots = jnp.dot(onehot[...], head, preferred_element_type=F32) + jnp.dot(
        onehot[...], rest, preferred_element_type=F32
    )
    s2[...] = in_slots.reshape(8, 64, 128)
    copies2 = send(FAR_FIRST, q, 8, q_device, lambda to: s2.at[to], lambda d: r2.at[d], sem2)
    arrive(copies2)
    total = s2[q]
    for d in range(1, 8):
        total = total + r2[d]

    s3[...] = total.reshape(8, 8, 128)
    copies3 = send(FAR_FIRST, z, 8, z_device, lambda to: s3.at[to], lambda d: r3.at[z], sem3)
    r3[z] = s3[z]
    leg_copy.wait()
    tail[0:8, :] = leg[8192:8200, :].astype(F32)
    arrive(copies3)
    for r in range(2):
        for o in range(2):
            j = 2 * o + r
            for h in range(2):
                cols = slice(128 * h, 128 * h + 128)
                tile = turned(r3[4 * h], -32 * j)
                for g in range(1, 4):
                    tile = jnp.where(quarter == g, turned(r3[4 * h + g], 32 * (g - j)), tile)
                at = 16 * r + 8 * o
                four[at:at + 8, cols] = tile / float(TOTAL_LON) * quad[0:1, cols]
    fourier = four[...].astype(BF16)

    own_slot = lane % 8 == tile_row
    low_limit = DEGREES - pair_int - step_in_tile
    tail_rows = tail[...].astype(BF16)

    def row_of(t):
        return (t % 8) * 8 + t // 8

    for base in range(0, 64, 8):
        product = lax.dot_general(
            fourier, leg[128 * base:128 * base + 1024, :], (((1,), (1,)), ((), ())), preferred_element_type=F32
        )
        for t in range(base, base + 8):
            piece = product[:, 128 * (t - base):128 * (t - base) + 128]
            is_low = jnp.broadcast_to(16 * t < low_limit, (8, 128))
            chunk, row = divmod(row_of(t), 16)
            for r in range(2):
                picked = jnp.where(is_low, piece[16 * r:16 * r + 8], piece[16 * r + 8:16 * r + 16])
                summed = jnp.sum(jnp.where(own_slot, picked, 0.0), axis=0, keepdims=True)
                s4[chunk, 16 * r + row:16 * r + row + 1, :] = summed
    product = lax.dot_general(fourier, tail_rows, (((1,), (1,)), ((), ())), preferred_element_type=F32)
    for r in range(2):
        summed = jnp.sum(jnp.where(own_slot, product[16 * r + 8:16 * r + 16], 0.0), axis=0, keepdims=True)
        for chunk in range(4):
            s4[chunk, 32 + r:33 + r, :] = summed

    copies4 = send((2, 1, 3), x, 4, x_device, lambda to: s4.at[to], lambda d: r4.at[d], sem4)
    arrive(copies4)
    total = s4[x] + r4[1] + r4[2] + r4[3]
    own_factor = factor[pl.ds(pl.multiple_of(16 * x, 16), 16), :]
    scaled = jnp.concatenate([total[0:16] * own_factor, total[16:32] * own_factor], axis=0)
    r5[x] = scaled.astype(BF16)
    copies5 = send((2, 1, 3), x, 4, x_device, lambda to: r5.at[x], lambda d: r5.at[x], sem5)
    last_scaled = (total[32:40] * factor[64:65, :]).astype(BF16).astype(F32)
    arrive(copies5)

    for chunk in range(4):
        spectral = r5[chunk].astype(F32)
        for row in range(16):
            t0, t1 = divmod(16 * chunk + row, 8)
            t = 8 * t1 + t0
            is_low = jnp.broadcast_to(16 * t < low_limit, (8, 128))
            pieces = []
            for r in range(2):
                line = jnp.broadcast_to(spectral[16 * r + row:16 * r + row + 1], (8, 128))
                line = jnp.where(own_slot, line, 0.0)
                pieces += [jnp.where(is_low, line, 0.0), jnp.where(is_low, 0.0, line)]
            blocks[:, 128 * t:128 * t + 128] = jnp.concatenate(pieces, axis=0).astype(BF16)
    pieces = []
    for r in range(2):
        line = jnp.where(own_slot, jnp.broadcast_to(last_scaled[r:r + 1], (8, 128)), 0.0)
        pieces += [jnp.zeros((8, 128), F32), line]
    profile = jnp.dot(jnp.concatenate(pieces, axis=0).astype(BF16), tail_rows, preferred_element_type=F32)
    for base in range(0, 8192, 1024):
        profile = profile + jnp.dot(
            blocks[:, base:base + 1024], leg[base:base + 1024, :], preferred_element_type=F32
        )
    profile = profile.astype(BF16).astype(F32)

    for h in range(2):
        for g in range(4):
            tile = turned(profile[0:8, 128 * h:128 * h + 128], -32 * g)
            for j in range(1, 4):
                at = 16 * (j % 2) + 8 * (j // 2)
                tile = jnp.where(
                    quarter == j, turned(profile[at:at + 8, 128 * h:128 * h + 128], 32 * (j - g)), tile
                )
            s6[4 * h + g] = tile
    copies6 = send(FAR_FIRST, z, 8, z_device, lambda to: s6.at[to], lambda d: r6.at[z], sem6)
    r6[z] = s6[z]
    arrive(copies6)

    r7[q] = r6[...].reshape(64, 128).astype(BF16)
    copies7 = send(FAR_FIRST, q, 8, q_device, lambda to: r7.at[q], lambda d: r7.at[q], sem7)
    arrive(copies7)
    natural = lax.dot_general(
        r7[...].reshape(512, 128), onehot[...], (((0,), (0,)), ((), ())), preferred_element_type=F32
    )
    wide_lane = lax.broadcasted_iota(jnp.int32, (1, 256), 1)
    second_half = wide_lane % 128 >= 64
    waves = []
    for g in range(4):
        low = slice(128 * g, 128 * g + 128)
        high = slice(512 + 128 * g, 640 + 128 * g)
        re = jnp.concatenate([natural[0:32, low], natural[64:96, high]], axis=1)
        im = jnp.concatenate([natural[32:64, low], natural[96:128, high]], axis=1)
        if g:
            left = jnp.concatenate([re, jnp.where(second_half, -im, im)], axis=0)
        else:
            re = jnp.where(wide_lane == 0, 0.5 * re, re)
            im = jnp.where(wide_lane == 0, 0.5 * im, im)
            left = jnp.concatenate([
                jnp.where(second_half, 0.0, re), jnp.where(second_half, 0.0, im),
                jnp.where(second_half, re, 0.0), jnp.where(second_half, im, 0.0),
            ], axis=0)
        left = left.astype(BF16)
        by_cos = jnp.dot(left, table[g, 0, 0:256], preferred_element_type=F32) + jnp.dot(
            left, table[g, 1, 0:256], preferred_element_type=F32
        )
        by_sin = jnp.dot(left, table[g, 0, 256:512], preferred_element_type=F32) + jnp.dot(
            left, table[g, 1, 256:512], preferred_element_type=F32
        )
        if g:
            waves.append((by_cos[0:32] - by_sin[32:64], by_sin[0:32] + by_cos[32:64]))
        else:
            waves.append((by_cos[0:32] - by_sin[32:64], by_cos[64:96] - by_sin[96:128]))
    (w0, w4), (re1, im1), (re2, im2), (re3, im3) = waves
    even0, even1 = w0 + w4, w0 - w4
    re_sum, re_dif = re1 + re3, root * (re1 - re3)
    im_dif, im_sum = im1 - im3, root * (im1 + im3)
    b0, b1, b2, b3 = even0 + re2, even1 - im2, even0 - re2, even1 + im2
    a0, a1, a2, a3 = re_sum, re_dif - im_sum, -im_dif, -re_dif - im_sum
    for i, value in enumerate((b0 + a0, b1 + a1, b2 + a2, b3 + a3, b0 - a0, b1 - a1, b2 - a2, b3 - a3)):
        s8[i] = (2.0 * value).astype(BF16)

    copies8 = send(FAR_FIRST, z, 8, z_device, lambda to: s8.at[to], lambda d: r8.at[z], sem8)
    r8[z] = s8[z]
    arrive(copies8)
    grid = r8[...].reshape(256, 256).astype(F32).T
    out[...] = grid[0:135, :]
    for copy in started:
        copy.wait_send()


def per_device(field, quad_weight, legendre, love_factor, pair_table):
    low, high = pair_orders()
    perm = np.broadcast_to(np.concatenate([low, high]).astype(np.float32), (8, 1024))
    pair_rows = jnp.broadcast_to(jnp.tile(pair_table.astype(F32), 16), (8, 128))
    vmem = pl.BlockSpec(memory_space=pltpu.VMEM)
    anywhere = pl.BlockSpec(memory_space=pl.ANY)
    pair_sems = pltpu.SemaphoreType.DMA((2, 8))
    grid = pl.pallas_call(
        kernel,
        out_shape=jax.ShapeDtypeStruct((LON_COLS, 256), F32),
        in_specs=[vmem] * 5 + [anywhere] * 2,
        out_specs=vmem,
        scratch_shapes=[
            pltpu.VMEM((8200, 256), BF16),
            pltpu.VMEM((4, 2, 512, 256), BF16),
            pltpu.VMEM((128, 256), F32),
            pltpu.VMEM((40, 256), F32),
            pltpu.VMEM((8, 40, 128), F32),
            pltpu.VMEM((8, 40, 128), F32),
            pltpu.VMEM((8, 8, 128), F32),
            pltpu.VMEM((64, 128), F32),
            pltpu.VMEM((512, 1024), BF16),
            pltpu.VMEM((4, 256, 128), F32),
            pltpu.VMEM((1024, 128), F32),
            pltpu.VMEM((8, 64, 128), F32),
            pltpu.VMEM((8, 64, 128), F32),
            pltpu.VMEM((8, 8, 128), F32),
            pltpu.VMEM((8, 8, 128), F32),
            pltpu.VMEM((32, 256), F32),
            pltpu.VMEM((4, 40, 128), F32),
            pltpu.VMEM((4, 40, 128), F32),
            pltpu.VMEM((4, 32, 128), BF16),
            pltpu.VMEM((72, 128), F32),
            pltpu.VMEM((16, 128), F32),
            pltpu.VMEM((32, 8192), BF16),
            pltpu.VMEM((8, 8, 128), F32),
            pltpu.VMEM((8, 8, 128), F32),
            pltpu.VMEM((8, 64, 128), BF16),
            pltpu.VMEM((8, 32, 256), BF16),
            pltpu.VMEM((8, 32, 256), BF16),
            pltpu.SemaphoreType.DMA((2,)),
        ] + [pair_sems] * 10,
        compiler_params=pltpu.CompilerParams(
            collective_id=0, has_side_effects=True, vmem_limit_bytes=40 * 1024 * 1024
        ),
    )(
        field.T,
        quad_weight.reshape(1, 256),
        love_factor.reshape(8, 128),
        pair_rows,
        jnp.asarray(perm),
        legendre.transpose(1, 0, 2).reshape(8200, 256),
        jnp.asarray(angle_constants()),
    )
    return grid.T


def solution(mesh):
    placed = (P("lat", "lon"), P("lat"), P("lon", None, "lat"), P(), P("lon"))
    return jax.shard_map(
        per_device, mesh=mesh, in_specs=placed, out_specs=P("lat", "lon"), check_vma=False
    )
```

```python
import math

import jax
import jax.numpy as jnp
import ml_dtypes
import numpy as np
from jax import lax
from jax.experimental import pallas as pl
from jax.experimental.pallas import tpu as pltpu
from jax.sharding import PartitionSpec as P

F32 = jnp.float32
BF16 = jnp.bfloat16
TOTAL_LON = 8640
LON_COLS = 135
DEGREES = 1024
GROUPS = ((0, 4), (1, 7), (2, 6), (3, 5))
FAR_FIRST = (4, 3, 5, 2, 6, 1, 7)


def pair_orders():
    steps = 8 * np.arange(64)
    low = np.concatenate([steps + r for group in GROUPS for r in group])
    high = np.concatenate([steps + 7 - r for group in GROUPS for r in group])
    return low, high


def angle_constants():
    low, high = pair_orders()
    columns = np.arange(LON_COLS)
    made = np.zeros((8, 4, 2, 512, 256), ml_dtypes.bfloat16)
    for group in range(4):
        span = slice(128 * group, 128 * group + 128)
        orders = np.concatenate([low[span], DEGREES - 1 - high[span]])
        sign = np.ones((256, 1))
        if group:
            sign[64:128] = -1.0
            sign[192:256] = -1.0
        for q in range(8):
            turns = orders[:, None] * (LON_COLS * q + columns) % TOTAL_LON
            angle = turns * (2.0 * np.pi / TOTAL_LON)
            both = np.concatenate([np.cos(angle), np.sin(angle) * sign])
            head = both.astype(ml_dtypes.bfloat16)
            made[q, group, 0, :, :LON_COLS] = head
            made[q, group, 1, :, :LON_COLS] = (both - head.astype(np.float64)).astype(ml_dtypes.bfloat16)
    return made


def kernel(
    field_in, quad_in, love_in, pair_in, legendre, angles, out,
    field, quad, love, pair_own, pairs, leg, table, tail, last_rows, s1, r1, rp1, rp2, onehot, rhs, orders_all, s2, r2, s3, r3, four, s4, r4, r5,
    factor, love_rows, blocks, s6, r6, r7, s8, r8,
    local_sem, sem_pz, sem_pq, sem1, sem2, sem3, sem4, sem5, sem6, sem7, sem8,
):
    lon = lax.axis_index("lon")
    x = lax.axis_index("lat")
    z = lon // 8
    q = lon % 8

    def z_device(i):
        return {"lon": i * 8 + q}

    def q_device(i):
        return {"lon": z * 8 + i}

    def x_device(i):
        return {"lat": i}

    barrier = pltpu.get_barrier_semaphore()
    for d in range(1, 8):
        pl.semaphore_signal(barrier, inc=1, device_id=z_device((z + d) % 8))
        pl.semaphore_signal(barrier, inc=1, device_id=q_device((q + d) % 8))
    for d in range(1, 4):
        pl.semaphore_signal(barrier, inc=1, device_id=x_device((x + d) % 4))

    field_copy = pltpu.make_async_copy(field_in, field, local_sem.at[2])
    pair_copy = pltpu.make_async_copy(pair_in, pair_own, local_sem.at[3])
    love_copy = pltpu.make_async_copy(love_in, love, local_sem.at[4])
    quad_copy = pltpu.make_async_copy(quad_in, quad, local_sem.at[5])
    leg_copy = pltpu.make_async_copy(legendre, leg, local_sem.at[0])
    table_copy = pltpu.make_async_copy(angles.at[q], table, local_sem.at[1])
    for copy in (pair_copy, field_copy, love_copy, quad_copy, table_copy, leg_copy):
        copy.start()

    started = []

    def send(distances, me, size, device, source, target, sems):
        copies = []
        for d in distances:
            to = (me + d) % size
            copy = pltpu.make_async_remote_copy(
                src_ref=source(to, d), dst_ref=target(d),
                send_sem=sems.at[0, d], recv_sem=sems.at[1, d],
                device_id=device(to),
            )
            copy.start()
            copies.append(copy)
        started.extend(copies)
        return copies

    def arrive(copies):
        for copy in copies:
            copy.wait_recv()

    lane = lax.broadcasted_iota(jnp.int32, (1, 128), 1)
    quarter = lane // 32
    step_in_tile = lane // 8

    last_rows[...] = jnp.zeros_like(last_rows)
    pair_copy.wait()
    spread = jnp.concatenate([pair_own[...].astype(F32), jnp.zeros((1, 120), F32)], axis=1)
    for shift in (8, 16, 32, 64):
        spread = spread + pltpu.roll(spread, shift, 1)
    pairs[...] = jnp.broadcast_to(spread, (8, 128))
    field_copy.wait()
    last_rows[0:15, :] = field[120:135, :]
    for h in range(2):
        cols = slice(128 * h, 128 * h + 128)
        runs = [field[40 * c:40 * c + 40, cols] for c in range(3)] + [last_rows[:, cols]]
        for g in range(4):
            packed = pltpu.roll(runs[0], (32 * (0 - g)) % 128, 1) if g else runs[0]
            for c in range(1, 4):
                moved = pltpu.roll(runs[c], (32 * (c - g)) % 128, 1) if c != g else runs[c]
                packed = jnp.where(quarter == c, moved, packed)
            s1[4 * h + g] = packed

    pl.semaphore_wait(barrier, 17)
    copies_pz = send(FAR_FIRST, z, 8, z_device, lambda to, d: pairs, lambda d: rp1.at[z], sem_pz)
    copies1 = send(FAR_FIRST, z, 8, z_device, lambda to, d: s1.at[to], lambda d: r1.at[z], sem1)
    r1[z] = s1[z]
    rp1[z] = pairs[...]

    tile_row = lax.broadcasted_iota(jnp.int32, (8, 128), 0)
    rhs[...] = jnp.zeros_like(rhs)
    s4[...] = jnp.zeros_like(s4)
    tail[...] = jnp.zeros_like(tail)
    love_rows[...] = jnp.zeros_like(love_rows)
    arrive(copies_pz)
    gathered = rp1[0]
    for i in range(1, 8):
        gathered = jnp.where(tile_row == i, rp1[i], gathered)
    mine = pl.ds(pl.multiple_of(8 * q, 8), 8)
    rp2[mine, :] = gathered
    copies_pq = send(FAR_FIRST, q, 8, q_device, lambda to, d: rp2.at[mine], lambda d: rp2.at[mine], sem_pq)

    pair_lane = pairs[0:1, :]
    love_copy.wait()
    love_rows[1:9, :] = love[...]
    love16 = love_rows[...]
    lane_row = lax.broadcasted_iota(jnp.int32, (128, 128), 0).astype(F32)
    step_f = step_in_tile.astype(F32)

    def shifted_love(start):
        whole = jnp.floor(start * (1.0 / 128.0))
        picked = jnp.where(lane_row == start - 128.0 * whole, 1.0, 0.0).astype(F32)
        rows = jnp.dot(love16, picked, preferred_element_type=F32, precision=lax.Precision.HIGHEST)
        for bit in (4, 2, 1):
            half = jnp.floor(whole * (1.0 / bit))
            odd = half - 2.0 * jnp.floor(half * 0.5)
            rows = jnp.where(odd > 0.5, pltpu.roll(rows, 16 - bit, 0), rows)
        return rows

    def column_ids(t0):
        return 128 * tile_row + (16 * t0 + step_in_tile)

    pair_int = pair_lane.astype(jnp.int32)
    for t0 in range(8):
        low_love = shifted_love(step_f + (pair_lane + (16.0 * t0 + 128.0)))
        high_love = shifted_love(step_f + (16.0 * t0 + 127.0))
        is_low = column_ids(t0) < DEGREES - pair_int
        factor[pl.ds(t0, 8, stride=8), :] = jnp.where(is_low, low_love[0:8], high_love[0:8])
        if t0 == 0:
            factor[64:72, :] = high_love[8:16]

    place = lax.broadcasted_iota(jnp.int32, (1, 1024), 1)
    group = place % 512 // 128
    other = jnp.where(group == 0, 4, 8 - group)
    residue = jnp.where(place % 128 < 64, group, other)
    wanted = (8 * (place % 64) + jnp.where(place < 512, residue, 7 - residue)).astype(F32)
    arrive(copies_pq)
    spread = jnp.broadcast_to(rp2[...].reshape(64, 1, 128), (64, 8, 128))
    diagonal = (tile_row == lane).reshape(1, 8, 128)
    column = jnp.sum(jnp.where(diagonal, spread, 0.0), axis=2, keepdims=True).reshape(512, 1)
    onehot[...] = jnp.where(column == wanted, 1.0, 0.0).astype(BF16)

    table_copy.wait()
    arrive(copies1)
    f = [r1[i] for i in range(8)]
    a = [f[i] - f[i + 4] for i in range(4)]
    b = [f[i] + f[i + 4] for i in range(4)]
    root = math.sqrt(0.5)
    a13m = root * (a[1] - a[3])
    a13p = root * (a[1] + a[3])
    parts = (
        (b[0] + b[1] + b[2] + b[3], b[0] - b[1] + b[2] - b[3]),
        (a[0] + a13m, -a[2] - a13p),
        (b[0] - b[2], b[3] - b[1]),
        (a[0] - a13m, a[2] - a13p),
    )

    def turned(value, by):
        return pltpu.roll(value, by % 128, value.ndim - 1) if by % 128 else value

    for g in range(4):
        re, im = parts[g]
        for c in range(4):
            rhs[g, 40 * c:40 * c + 40, :] = jnp.where(
                quarter < 2,
                jnp.where(quarter == 0, turned(re, -32 * c), turned(im, 32 - 32 * c)),
                jnp.where(quarter == 2, turned(re, 64 - 32 * c), turned(im, 96 - 32 * c)),
            )
    for g in range(4):
        value = rhs[g]
        head = value.astype(BF16).astype(F32)
        both = jnp.where(lane < 64, head, value - head).astype(BF16)
        first = jnp.dot(table[g, 0], both, preferred_element_type=F32)
        second = jnp.dot(table[g, 1], both, preferred_element_type=F32)
        total = first + turned(first, 64) + second
        d1, d2 = total[0:256], total[256:512]
        if g:
            spectrum = d1 + jnp.where(quarter == 0, turned(d2, 96), -turned(d2, 32))
            flipped = jnp.where(quarter == 1, -spectrum, spectrum)
            rows = (spectrum[0:64], flipped[64:128], spectrum[128:192], flipped[192:256])
        else:
            plain = jnp.where(quarter == 0, d1, -turned(d2, 32))
            other = jnp.where(quarter == 0, turned(d1, 96), -d2)
            rows = (plain[0:64], other[64:128], plain[128:192], other[192:256])
        for half in range(2):
            at = 128 * g + 64 * half
            orders_all[at:at + 64, :] = jnp.where(lane < 64, rows[half], 0.0)
            orders_all[512 + at:512 + at + 64, :] = jnp.where(lane < 64, 0.0, turned(rows[2 + half], 64))
    value = orders_all[...]
    head = value.astype(BF16)
    rest = (value - head.astype(F32)).astype(BF16)
    copies2 = []
    for part in ((4, 3, 5, 2), (6, 1, 7, 0)):
        rows = jnp.concatenate(
            [onehot[pl.ds(pl.multiple_of((q + d) % 8 * 64, 64), 64), :] for d in part], axis=0
        )
        in_slots = jnp.dot(rows, head, preferred_element_type=F32) + jnp.dot(rows, rest, preferred_element_type=F32)
        for i, d in enumerate(part):
            s2[d] = in_slots[64 * i:64 * i + 64]
        copies2 += send(
            [d for d in part if d], q, 8, q_device, lambda to, d: s2.at[d], lambda d: r2.at[d], sem2
        )
    arrive(copies2)
    total = s2[0]
    for d in range(1, 8):
        total = total + r2[d]

    s3[...] = total.reshape(8, 8, 128)
    copies3 = send(FAR_FIRST, z, 8, z_device, lambda to, d: s3.at[to], lambda d: r3.at[z], sem3)
    r3[z] = s3[z]
    quad_copy.wait()
    leg_copy.wait()
    tail[0:8, :] = leg[8192:8200, :].astype(F32)
    arrive(copies3)
    for r in range(2):
        for o in range(2):
            j = 2 * o + r
            for h in range(2):
                cols = slice(128 * h, 128 * h + 128)
                tile = turned(r3[4 * h], -32 * j)
                for g in range(1, 4):
                    tile = jnp.where(quarter == g, turned(r3[4 * h + g], 32 * (g - j)), tile)
                at = 16 * r + 8 * o
                four[at:at + 8, cols] = tile / float(TOTAL_LON) * quad[0:1, cols]
    fourier = four[...].astype(BF16)

    own_slot = lane % 8 == tile_row
    low_limit = DEGREES - pair_int - step_in_tile
    tail_rows = tail[...].astype(BF16)

    def analysed(piece, is_low, r):
        if is_low is None:
            picked = piece[16 * r + 8:16 * r + 16]
        else:
            picked = jnp.where(is_low, piece[16 * r:16 * r + 8], piece[16 * r + 8:16 * r + 16])
        return jnp.sum(jnp.where(own_slot, picked, 0.0), axis=0, keepdims=True)

    def chunk_rows(chunk):
        return pl.ds(pl.multiple_of(2048 * chunk, 2048), 2048)

    product = lax.dot_general(fourier, tail_rows, (((1,), (1,)), ((), ())), preferred_element_type=F32)
    for r in range(2):
        summed = analysed(product, None, r)
        for d in range(4):
            s4[d, 32 + r:33 + r, :] = summed
    copies4 = []
    for d in (2, 1, 3, 0):
        chunk = (x + d) % 4
        product = lax.dot_general(
            fourier, leg[chunk_rows(chunk), :], (((1,), (1,)), ((), ())), preferred_element_type=F32
        )
        for row in range(16):
            is_low = jnp.broadcast_to(16 * (16 * chunk + row) < low_limit, (8, 128))
            for r in range(2):
                s4[d, 16 * r + row:16 * r + row + 1, :] = analysed(product[:, 128 * row:128 * row + 128], is_low, r)
        if d:
            copies4 += send((d,), x, 4, x_device, lambda to, d: s4.at[d], lambda d: r4.at[d], sem4)

    arrive(copies4)
    total = s4[0] + r4[1] + r4[2] + r4[3]
    own_factor = factor[pl.ds(pl.multiple_of(16 * x, 16), 16), :]
    scaled = jnp.concatenate([total[0:16] * own_factor, total[16:32] * own_factor], axis=0)
    r5[0] = scaled.astype(BF16)
    copies5 = send((2, 1, 3), x, 4, x_device, lambda to, d: r5.at[0], lambda d: r5.at[d], sem5)
    last_scaled = (total[32:40] * factor[64:65, :]).astype(BF16).astype(F32)

    pieces = []
    for r in range(2):
        line = jnp.where(own_slot, jnp.broadcast_to(last_scaled[r:r + 1], (8, 128)), 0.0)
        pieces += [jnp.zeros((8, 128), F32), line]
    profile = jnp.dot(jnp.concatenate(pieces, axis=0).astype(BF16), tail_rows, preferred_element_type=F32)
    for d in (0, 1, 3, 2):
        if d:
            arrive([copies5[(2, 1, 3).index(d)]])
        chunk = (x - d + 4) % 4
        spectral = r5[d].astype(F32)
        for row in range(16):
            is_low = jnp.broadcast_to(16 * (16 * chunk + row) < low_limit, (8, 128))
            pieces = []
            for r in range(2):
                line = jnp.broadcast_to(spectral[16 * r + row:16 * r + row + 1], (8, 128))
                line = jnp.where(own_slot, line, 0.0)
                pieces += [jnp.where(is_low, line, 0.0), jnp.where(is_low, 0.0, line)]
            blocks[d, :, 128 * row:128 * row + 128] = jnp.concatenate(pieces, axis=0).astype(BF16)
        profile = profile + jnp.dot(blocks[d], leg[chunk_rows(chunk), :], preferred_element_type=F32)
    profile = profile.astype(BF16).astype(F32)

    for h in range(2):
        for g in range(4):
            tile = turned(profile[0:8, 128 * h:128 * h + 128], -32 * g)
            for j in range(1, 4):
                at = 16 * (j % 2) + 8 * (j // 2)
                tile = jnp.where(
                    quarter == j, turned(profile[at:at + 8, 128 * h:128 * h + 128], 32 * (j - g)), tile
                )
            s6[4 * h + g] = tile
    copies6 = send(FAR_FIRST, z, 8, z_device, lambda to, d: s6.at[to], lambda d: r6.at[z], sem6)
    r6[z] = s6[z]
    arrive(copies6)

    r7[q] = r6[...].reshape(64, 128).astype(BF16)
    copies7 = send(FAR_FIRST, q, 8, q_device, lambda to, d: r7.at[q], lambda d: r7.at[q], sem7)
    arrive(copies7)
    natural = lax.dot_general(
        r7[...].reshape(512, 128), onehot[...], (((0,), (0,)), ((), ())), preferred_element_type=F32
    )
    wide_lane = lax.broadcasted_iota(jnp.int32, (1, 256), 1)
    second_half = wide_lane % 128 >= 64
    waves = []
    for g in range(4):
        low = slice(128 * g, 128 * g + 128)
        high = slice(512 + 128 * g, 640 + 128 * g)
        re = jnp.concatenate([natural[0:32, low], natural[64:96, high]], axis=1)
        im = jnp.concatenate([natural[32:64, low], natural[96:128, high]], axis=1)
        if g:
            left = jnp.concatenate([re, jnp.where(second_half, -im, im)], axis=0)
        else:
            re = jnp.where(wide_lane == 0, 0.5 * re, re)
            im = jnp.where(wide_lane == 0, 0.5 * im, im)
            left = jnp.concatenate([
                jnp.where(second_half, 0.0, re), jnp.where(second_half, 0.0, im),
                jnp.where(second_half, re, 0.0), jnp.where(second_half, im, 0.0),
            ], axis=0)
        left = left.astype(BF16)
        by_cos = jnp.dot(left, table[g, 0, 0:256], preferred_element_type=F32) + jnp.dot(
            left, table[g, 1, 0:256], preferred_element_type=F32
        )
        by_sin = jnp.dot(left, table[g, 0, 256:512], preferred_element_type=F32) + jnp.dot(
            left, table[g, 1, 256:512], preferred_element_type=F32
        )
        if g:
            waves.append((by_cos[0:32] - by_sin[32:64], by_sin[0:32] + by_cos[32:64]))
        else:
            waves.append((by_cos[0:32] - by_sin[32:64], by_cos[64:96] - by_sin[96:128]))
    (w0, w4), (re1, im1), (re2, im2), (re3, im3) = waves
    even0, even1 = w0 + w4, w0 - w4
    re_sum, re_dif = re1 + re3, root * (re1 - re3)
    im_dif, im_sum = im1 - im3, root * (im1 + im3)
    b0, b1, b2, b3 = even0 + re2, even1 - im2, even0 - re2, even1 + im2
    a0, a1, a2, a3 = re_sum, re_dif - im_sum, -im_dif, -re_dif - im_sum
    for i, value in enumerate((b0 + a0, b1 + a1, b2 + a2, b3 + a3, b0 - a0, b1 - a1, b2 - a2, b3 - a3)):
        s8[i] = (2.0 * value).astype(BF16)

    copies8 = send(FAR_FIRST, z, 8, z_device, lambda to, d: s8.at[to], lambda d: r8.at[z], sem8)
    r8[z] = s8[z]
    arrive(copies8)
    grid = r8[...].reshape(256, 256).astype(F32).T
    out[...] = grid[0:135, :]
    for copy in started:
        copy.wait_send()


def per_device(field, quad_weight, legendre, love_factor, pair_table):
    vmem = pl.BlockSpec(memory_space=pltpu.VMEM)
    anywhere = pl.BlockSpec(memory_space=pl.ANY)
    pair_sems = pltpu.SemaphoreType.DMA((2, 8))
    grid = pl.pallas_call(
        kernel,
        out_shape=jax.ShapeDtypeStruct((LON_COLS, 256), F32),
        in_specs=[anywhere] * 6,
        out_specs=vmem,
        scratch_shapes=[
            pltpu.VMEM((LON_COLS, 256), F32),
            pltpu.VMEM((1, 256), F32),
            pltpu.VMEM((8, 128), F32),
            pltpu.VMEM((1, 8), jnp.int32),
            pltpu.VMEM((8, 128), F32),
            pltpu.VMEM((8200, 256), BF16),
            pltpu.VMEM((4, 2, 512, 256), BF16),
            pltpu.VMEM((128, 256), F32),
            pltpu.VMEM((40, 256), F32),
            pltpu.VMEM((8, 40, 128), F32),
            pltpu.VMEM((8, 40, 128), F32),
            pltpu.VMEM((8, 8, 128), F32),
            pltpu.VMEM((64, 128), F32),
            pltpu.VMEM((512, 1024), BF16),
            pltpu.VMEM((4, 256, 128), F32),
            pltpu.VMEM((1024, 128), F32),
            pltpu.VMEM((8, 64, 128), F32),
            pltpu.VMEM((8, 64, 128), F32),
            pltpu.VMEM((8, 8, 128), F32),
            pltpu.VMEM((8, 8, 128), F32),
            pltpu.VMEM((32, 256), F32),
            pltpu.VMEM((4, 40, 128), F32),
            pltpu.VMEM((4, 40, 128), F32),
            pltpu.VMEM((4, 32, 128), BF16),
            pltpu.VMEM((72, 128), F32),
            pltpu.VMEM((16, 128), F32),
            pltpu.VMEM((4, 32, 2048), BF16),
            pltpu.VMEM((8, 8, 128), F32),
            pltpu.VMEM((8, 8, 128), F32),
            pltpu.VMEM((8, 64, 128), BF16),
            pltpu.VMEM((8, 32, 256), BF16),
            pltpu.VMEM((8, 32, 256), BF16),
            pltpu.SemaphoreType.DMA((6,)),
        ] + [pair_sems] * 10,
        compiler_params=pltpu.CompilerParams(
            collective_id=0, has_side_effects=True, vmem_limit_bytes=60 * 1024 * 1024
        ),
    )(
        field.T,
        quad_weight.reshape(1, 256),
        love_factor.reshape(8, 128),
        pair_table.reshape(1, 8),
        legendre.transpose(1, 0, 2).reshape(8200, 256),
        jnp.asarray(angle_constants()),
    )
    return grid.T


def solution(mesh):
    placed = (P("lat", "lon"), P("lat"), P("lon", None, "lat"), P(), P("lon"))
    return jax.shard_map(
        per_device, mesh=mesh, in_specs=placed, out_specs=P("lat", "lon"), check_vma=False
    )
```

```python
import math

import jax
import jax.numpy as jnp
import ml_dtypes
import numpy as np
from jax import lax
from jax.experimental import pallas as pl
from jax.experimental.pallas import tpu as pltpu
from jax.sharding import PartitionSpec as P

F32 = jnp.float32
BF16 = jnp.bfloat16
TOTAL_LON = 8640
LON_COLS = 135
DEGREES = 1024
GROUPS = ((0, 4), (1, 7), (2, 6), (3, 5))
FAR_FIRST = (4, 3, 5, 2, 6, 1, 7)


def pair_orders():
    steps = 8 * np.arange(64)
    low = np.concatenate([steps + r for group in GROUPS for r in group])
    high = np.concatenate([steps + 7 - r for group in GROUPS for r in group])
    return low, high


def angle_constants():
    low, high = pair_orders()
    columns = np.arange(LON_COLS)
    made = np.zeros((8, 4, 2, 512, 256), ml_dtypes.bfloat16)
    for group in range(4):
        span = slice(128 * group, 128 * group + 128)
        orders = np.concatenate([low[span], DEGREES - 1 - high[span]])
        sign = np.ones((256, 1))
        if group:
            sign[64:128] = -1.0
            sign[192:256] = -1.0
        for q in range(8):
            turns = orders[:, None] * (LON_COLS * q + columns) % TOTAL_LON
            angle = turns * (2.0 * np.pi / TOTAL_LON)
            both = np.concatenate([np.cos(angle), np.sin(angle) * sign])
            head = both.astype(ml_dtypes.bfloat16)
            made[q, group, 0, :, :LON_COLS] = head
            made[q, group, 1, :, :LON_COLS] = (both - head.astype(np.float64)).astype(ml_dtypes.bfloat16)
    return made


def kernel(
    field_in, quad_in, love_in, pair_in, legendre, angles, out,
    field, quad, love, pair_own, pairs, leg, table, tail, last_rows, s1, r1, rp1, rp2, onehot, rhs, orders_all, s2, r2, s3, r3, four, s4, r4,
    factor, love_rows, blocks, s6, r6, r7, s8,
    local_sem, sem_pz, sem_pq, sem1, sem2, sem3, sem6, sem7, sem8, sem4,
):
    lon = lax.axis_index("lon")
    x = lax.axis_index("lat")
    z = lon // 8
    q = lon % 8

    def z_device(i):
        return {"lon": i * 8 + q}

    def q_device(i):
        return {"lon": z * 8 + i}

    def x_device(i):
        return {"lat": i}

    barrier = pltpu.get_barrier_semaphore()
    for d in FAR_FIRST:
        pl.semaphore_signal(barrier, inc=1, device_id=z_device((z + d) % 8))
    for d in FAR_FIRST:
        pl.semaphore_signal(barrier, inc=1, device_id=q_device((q + d) % 8))
    for d in range(1, 4):
        pl.semaphore_signal(barrier, inc=1, device_id=x_device((x + d) % 4))

    field_copy = pltpu.make_async_copy(field_in, field, local_sem.at[2])
    pair_copy = pltpu.make_async_copy(pair_in, pair_own, local_sem.at[3])
    love_copy = pltpu.make_async_copy(love_in, love, local_sem.at[4])
    quad_copy = pltpu.make_async_copy(quad_in, quad, local_sem.at[5])
    leg_copy = pltpu.make_async_copy(legendre, leg, local_sem.at[0])
    table_copy = pltpu.make_async_copy(angles.at[q], table, local_sem.at[1])
    for copy in (pair_copy, field_copy, love_copy, quad_copy, table_copy, leg_copy):
        copy.start()

    unsettled = []

    def send(distances, me, size, device, source, target, sems):
        copies = []
        for d in distances:
            to = (me + d) % size
            copy = pltpu.make_async_remote_copy(
                src_ref=source(to, d), dst_ref=target(d),
                send_sem=sems.at[0, d], recv_sem=sems.at[1, d],
                device_id=device(to),
            )
            copy.start()
            copies.append(copy)
        unsettled.extend(copies)
        return copies

    def settle(keep=0):
        while len(unsettled) > keep:
            unsettled.pop(0).wait_send()

    def arrive(copies):
        for copy in copies:
            copy.wait_recv()

    lane = lax.broadcasted_iota(jnp.int32, (1, 128), 1)
    quarter = lane // 32
    step_in_tile = lane // 8

    last_rows[...] = jnp.zeros_like(last_rows)
    pair_copy.wait()
    spread = jnp.concatenate([pair_own[...].astype(F32), jnp.zeros((1, 120), F32)], axis=1)
    for shift in (8, 16, 32, 64):
        spread = spread + pltpu.roll(spread, shift, 1)
    pairs[...] = jnp.broadcast_to(spread, (8, 128))
    field_copy.wait()
    last_rows[0:15, :] = field[120:135, :]
    for h in range(2):
        cols = slice(128 * h, 128 * h + 128)
        runs = [field[40 * c:40 * c + 40, cols] for c in range(3)] + [last_rows[:, cols]]
        for g in range(4):
            packed = pltpu.roll(runs[0], (32 * (0 - g)) % 128, 1) if g else runs[0]
            for c in range(1, 4):
                moved = pltpu.roll(runs[c], (32 * (c - g)) % 128, 1) if c != g else runs[c]
                packed = jnp.where(quarter == c, moved, packed)
            s1[4 * h + g] = packed

    pl.semaphore_wait(barrier, 17)
    copies_pq = send(FAR_FIRST, q, 8, q_device, lambda to, d: pairs, lambda d: rp1.at[q], sem_pq)
    copies1 = send(FAR_FIRST, z, 8, z_device, lambda to, d: s1.at[to], lambda d: r1.at[z], sem1)
    r1[z] = s1[z]
    rp1[q] = pairs[...]

    tile_row = lax.broadcasted_iota(jnp.int32, (8, 128), 0)
    rhs[...] = jnp.zeros_like(rhs)
    s4[...] = jnp.zeros_like(s4)
    tail[...] = jnp.zeros_like(tail)
    love_rows[...] = jnp.zeros_like(love_rows)
    arrive(copies_pq)
    gathered = rp1[0]
    for i in range(1, 8):
        gathered = jnp.where(tile_row == i, rp1[i], gathered)
    rp2[z] = gathered
    copies_pz = send(FAR_FIRST, z, 8, z_device, lambda to, d: rp2.at[z], lambda d: rp2.at[z], sem_pz)

    pair_lane = pairs[0:1, :]
    love_copy.wait()
    love_rows[1:9, :] = love[...]
    love16 = love_rows[...]
    lane_row = lax.broadcasted_iota(jnp.int32, (128, 128), 0).astype(F32)
    step_f = step_in_tile.astype(F32)

    def shifted_love(start):
        whole = jnp.floor(start * (1.0 / 128.0))
        picked = jnp.where(lane_row == start - 128.0 * whole, 1.0, 0.0).astype(F32)
        rows = jnp.dot(love16, picked, preferred_element_type=F32, precision=lax.Precision.HIGHEST)
        for bit in (4, 2, 1):
            half = jnp.floor(whole * (1.0 / bit))
            odd = half - 2.0 * jnp.floor(half * 0.5)
            rows = jnp.where(odd > 0.5, pltpu.roll(rows, 16 - bit, 0), rows)
        return rows

    def column_ids(t0):
        return 128 * tile_row + (16 * t0 + step_in_tile)

    pair_int = pair_lane.astype(jnp.int32)
    for t0 in range(8):
        low_love = shifted_love(step_f + (pair_lane + (16.0 * t0 + 128.0)))
        high_love = shifted_love(step_f + (16.0 * t0 + 127.0))
        is_low = column_ids(t0) < DEGREES - pair_int
        factor[pl.ds(t0, 8, stride=8), :] = jnp.where(is_low, low_love[0:8], high_love[0:8])
        if t0 == 0:
            factor[64:72, :] = high_love[8:16]

    place = lax.broadcasted_iota(jnp.int32, (1, 1024), 1)
    group = place % 512 // 128
    other = jnp.where(group == 0, 4, 8 - group)
    residue = jnp.where(place % 128 < 64, group, other)
    wanted = (8 * (place % 64) + jnp.where(place < 512, residue, 7 - residue)).astype(F32)
    arrive(copies_pz)
    spread = jnp.concatenate([rp2[:, i:i + 1, :] for i in range(8)], axis=0)
    spread = jnp.broadcast_to(spread, (64, 8, 128))
    diagonal = (tile_row == lane).reshape(1, 8, 128)
    column = jnp.sum(jnp.where(diagonal, spread, 0.0), axis=2, keepdims=True).reshape(512, 1)
    onehot[...] = jnp.where(column == wanted, 1.0, 0.0).astype(BF16)

    table_copy.wait()
    arrive(copies1)
    f = [r1[i] for i in range(8)]
    a = [f[i] - f[i + 4] for i in range(4)]
    b = [f[i] + f[i + 4] for i in range(4)]
    root = math.sqrt(0.5)
    a13m = root * (a[1] - a[3])
    a13p = root * (a[1] + a[3])
    parts = (
        (b[0] + b[1] + b[2] + b[3], b[0] - b[1] + b[2] - b[3]),
        (a[0] + a13m, -a[2] - a13p),
        (b[0] - b[2], b[3] - b[1]),
        (a[0] - a13m, a[2] - a13p),
    )

    def turned(value, by):
        return pltpu.roll(value, by % 128, value.ndim - 1) if by % 128 else value

    for g in range(4):
        re, im = parts[g]
        for c in range(4):
            rhs[g, 40 * c:40 * c + 40, :] = jnp.where(
                quarter < 2,
                jnp.where(quarter == 0, turned(re, -32 * c), turned(im, 32 - 32 * c)),
                jnp.where(quarter == 2, turned(re, 64 - 32 * c), turned(im, 96 - 32 * c)),
            )
    for g in range(4):
        value = rhs[g]
        head = value.astype(BF16).astype(F32)
        both = jnp.where(lane < 64, head, value - head).astype(BF16)
        first = jnp.dot(table[g, 0], both, preferred_element_type=F32)
        second = jnp.dot(table[g, 1], both, preferred_element_type=F32)
        total = first + turned(first, 64) + second
        d1, d2 = total[0:256], total[256:512]
        if g:
            spectrum = d1 + jnp.where(quarter == 0, turned(d2, 96), -turned(d2, 32))
            flipped = jnp.where(quarter == 1, -spectrum, spectrum)
            rows = (spectrum[0:64], flipped[64:128], spectrum[128:192], flipped[192:256])
        else:
            plain = jnp.where(quarter == 0, d1, -turned(d2, 32))
            other = jnp.where(quarter == 0, turned(d1, 96), -d2)
            rows = (plain[0:64], other[64:128], plain[128:192], other[192:256])
        for half in range(2):
            at = 128 * g + 64 * half
            orders_all[at:at + 64, :] = jnp.where(lane < 64, rows[half], 0.0)
            orders_all[512 + at:512 + at + 64, :] = jnp.where(lane < 64, 0.0, turned(rows[2 + half], 64))
    value = orders_all[...]
    head = value.astype(BF16)
    rest = (value - head.astype(F32)).astype(BF16)
    copies2 = []
    for part in ((4, 3, 5, 2), (6, 1, 7, 0)):
        rows = jnp.concatenate(
            [onehot[pl.ds(pl.multiple_of((q + d) % 8 * 64, 64), 64), :] for d in part], axis=0
        )
        in_slots = jnp.dot(rows, head, preferred_element_type=F32) + jnp.dot(rows, rest, preferred_element_type=F32)
        for i, d in enumerate(part):
            s2[d] = in_slots[64 * i:64 * i + 64]
        copies2 += send(
            [d for d in part if d], q, 8, q_device, lambda to, d: s2.at[d], lambda d: r2.at[d], sem2
        )
    settle(7)
    arrive(copies2)
    total = s2[0]
    for d in range(1, 8):
        total = total + r2[d]

    s3[...] = total.reshape(8, 8, 128)
    copies3 = send(FAR_FIRST, z, 8, z_device, lambda to, d: s3.at[to], lambda d: r3.at[z], sem3)
    r3[z] = s3[z]
    quad_copy.wait()
    leg_copy.wait()
    tail[0:8, :] = leg[8192:8200, :].astype(F32)
    settle(7)
    arrive(copies3)
    for r in range(2):
        for o in range(2):
            j = 2 * o + r
            for h in range(2):
                cols = slice(128 * h, 128 * h + 128)
                tile = turned(r3[4 * h], -32 * j)
                for g in range(1, 4):
                    tile = jnp.where(quarter == g, turned(r3[4 * h + g], 32 * (g - j)), tile)
                at = 16 * r + 8 * o
                four[at:at + 8, cols] = tile / float(TOTAL_LON) * quad[0:1, cols]
    fourier = four[...].astype(BF16)

    own_slot = lane % 8 == tile_row
    low_limit = DEGREES - pair_int - step_in_tile
    tail_rows = tail[...].astype(BF16)

    def analysed(piece, is_low, r):
        if is_low is None:
            picked = piece[16 * r + 8:16 * r + 16]
        else:
            picked = jnp.where(is_low, piece[16 * r:16 * r + 8], piece[16 * r + 8:16 * r + 16])
        return jnp.sum(jnp.where(own_slot, picked, 0.0), axis=0, keepdims=True)

    product = lax.dot_general(fourier, tail_rows, (((1,), (1,)), ((), ())), preferred_element_type=F32)
    for r in range(2):
        s4[0, 32 + r:33 + r, :] = analysed(product, None, r)
    copies4 = []
    for chunk in range(4):
        product = lax.dot_general(
            fourier, leg[2048 * chunk:2048 * chunk + 2048, :], (((1,), (1,)), ((), ())), preferred_element_type=F32
        )
        for row in range(16):
            is_low = jnp.broadcast_to(16 * (16 * chunk + row) < low_limit, (8, 128))
            for r in range(2):
                s4[chunk, 16 * r + row:16 * r + row + 1, :] = analysed(
                    product[:, 128 * row:128 * row + 128], is_low, r
                )
        size = 32 if chunk else 40
        copies4.append(send(
            (2, 1, 3), x, 4, x_device,
            lambda to, d: s4.at[chunk, pl.ds(0, size)], lambda d: r4.at[d, chunk, pl.ds(0, size)], sem4.at[chunk],
        ))

    settle(12)
    profile = jnp.zeros((32, 256), F32)
    for chunk in range(4):
        arrive(copies4[chunk])
        total = s4[chunk] + r4[1, chunk] + r4[2, chunk] + r4[3, chunk]
        scale = factor[16 * chunk:16 * chunk + 16, :]
        spectral = jnp.concatenate([total[0:16] * scale, total[16:32] * scale], axis=0).astype(BF16).astype(F32)
        for row in range(16):
            is_low = jnp.broadcast_to(16 * (16 * chunk + row) < low_limit, (8, 128))
            pieces = []
            for r in range(2):
                line = jnp.broadcast_to(spectral[16 * r + row:16 * r + row + 1], (8, 128))
                line = jnp.where(own_slot, line, 0.0)
                pieces += [jnp.where(is_low, line, 0.0), jnp.where(is_low, 0.0, line)]
            blocks[chunk, :, 128 * row:128 * row + 128] = jnp.concatenate(pieces, axis=0).astype(BF16)
        profile = profile + jnp.dot(
            blocks[chunk], leg[2048 * chunk:2048 * chunk + 2048, :], preferred_element_type=F32
        )
        if chunk == 0:
            last = (total[32:40] * factor[64:65, :]).astype(BF16).astype(F32)
            pieces = []
            for r in range(2):
                line = jnp.where(own_slot, jnp.broadcast_to(last[r:r + 1], (8, 128)), 0.0)
                pieces += [jnp.zeros((8, 128), F32), line]
            profile = profile + jnp.dot(
                jnp.concatenate(pieces, axis=0).astype(BF16), tail_rows, preferred_element_type=F32
            )
    profile = profile.astype(BF16).astype(F32)

    for h in range(2):
        for g in range(4):
            tile = turned(profile[0:8, 128 * h:128 * h + 128], -32 * g)
            for j in range(1, 4):
                at = 16 * (j % 2) + 8 * (j // 2)
                tile = jnp.where(
                    quarter == j, turned(profile[at:at + 8, 128 * h:128 * h + 128], 32 * (j - g)), tile
                )
            s6[4 * h + g] = tile
    copies6 = send(FAR_FIRST, z, 8, z_device, lambda to, d: s6.at[to], lambda d: r6.at[z], sem6)
    r6[z] = s6[z]
    settle(7)
    arrive(copies6)

    r7[q] = r6[...].reshape(64, 128).astype(BF16)
    copies7 = send(FAR_FIRST, q, 8, q_device, lambda to, d: r7.at[q], lambda d: r7.at[q], sem7)
    settle(7)
    arrive(copies7)
    natural = lax.dot_general(
        r7[...].reshape(512, 128), onehot[...], (((0,), (0,)), ((), ())), preferred_element_type=F32
    )
    wide_lane = lax.broadcasted_iota(jnp.int32, (1, 256), 1)
    second_half = wide_lane % 128 >= 64
    waves = []
    for g in range(4):
        low = slice(128 * g, 128 * g + 128)
        high = slice(512 + 128 * g, 640 + 128 * g)
        re = jnp.concatenate([natural[0:32, low], natural[64:96, high]], axis=1)
        im = jnp.concatenate([natural[32:64, low], natural[96:128, high]], axis=1)
        if g:
            left = jnp.concatenate([re, jnp.where(second_half, -im, im)], axis=0)
        else:
            re = jnp.where(wide_lane == 0, 0.5 * re, re)
            im = jnp.where(wide_lane == 0, 0.5 * im, im)
            left = jnp.concatenate([
                jnp.where(second_half, 0.0, re), jnp.where(second_half, 0.0, im),
                jnp.where(second_half, re, 0.0), jnp.where(second_half, im, 0.0),
            ], axis=0)
        left = left.astype(BF16)
        by_cos = jnp.dot(left, table[g, 0, 0:256], preferred_element_type=F32) + jnp.dot(
            left, table[g, 1, 0:256], preferred_element_type=F32
        )
        by_sin = jnp.dot(left, table[g, 0, 256:512], preferred_element_type=F32) + jnp.dot(
            left, table[g, 1, 256:512], preferred_element_type=F32
        )
        if g:
            waves.append((by_cos[0:32] - by_sin[32:64], by_sin[0:32] + by_cos[32:64]))
        else:
            waves.append((by_cos[0:32] - by_sin[32:64], by_cos[64:96] - by_sin[96:128]))
    (w0, w4), (re1, im1), (re2, im2), (re3, im3) = waves
    even0, even1 = w0 + w4, w0 - w4
    re_sum, re_dif = re1 + re3, root * (re1 - re3)
    im_dif, im_sum = im1 - im3, root * (im1 + im3)
    b0, b1, b2, b3 = even0 + re2, even1 - im2, even0 - re2, even1 + im2
    a0, a1, a2, a3 = re_sum, re_dif - im_sum, -im_dif, -re_dif - im_sum
    for i, value in enumerate((b0 + a0, b1 + a1, b2 + a2, b3 + a3, b0 - a0, b1 - a1, b2 - a2, b3 - a3)):
        s8[i] = (2.0 * value).astype(BF16)

    copies8 = send(FAR_FIRST, z, 8, z_device, lambda to, d: s8.at[to], lambda d: out.at[z], sem8)
    own_copy = pltpu.make_async_copy(s8.at[z], out.at[z], local_sem.at[6])
    own_copy.start()
    settle(7)
    arrive(copies8)
    own_copy.wait()
    settle()


def per_device(field, quad_weight, legendre, love_factor, pair_table):
    anywhere = pl.BlockSpec(memory_space=pl.ANY)
    pair_sems = pltpu.SemaphoreType.DMA((2, 8))
    grid = pl.pallas_call(
        kernel,
        out_shape=jax.ShapeDtypeStruct((8, 32, 256), BF16),
        in_specs=[anywhere] * 6,
        out_specs=anywhere,
        scratch_shapes=[
            pltpu.VMEM((LON_COLS, 256), F32),
            pltpu.VMEM((1, 256), F32),
            pltpu.VMEM((8, 128), F32),
            pltpu.VMEM((1, 8), jnp.int32),
            pltpu.VMEM((8, 128), F32),
            pltpu.VMEM((8200, 256), BF16),
            pltpu.VMEM((4, 2, 512, 256), BF16),
            pltpu.VMEM((128, 256), F32),
            pltpu.VMEM((40, 256), F32),
            pltpu.VMEM((8, 40, 128), F32),
            pltpu.VMEM((8, 40, 128), F32),
            pltpu.VMEM((8, 8, 128), F32),
            pltpu.VMEM((8, 8, 128), F32),
            pltpu.VMEM((512, 1024), BF16),
            pltpu.VMEM((4, 256, 128), F32),
            pltpu.VMEM((1024, 128), F32),
            pltpu.VMEM((8, 64, 128), F32),
            pltpu.VMEM((8, 64, 128), F32),
            pltpu.VMEM((8, 8, 128), F32),
            pltpu.VMEM((8, 8, 128), F32),
            pltpu.VMEM((32, 256), F32),
            pltpu.VMEM((4, 40, 128), F32),
            pltpu.VMEM((4, 4, 40, 128), F32),
            pltpu.VMEM((72, 128), F32),
            pltpu.VMEM((16, 128), F32),
            pltpu.VMEM((4, 32, 2048), BF16),
            pltpu.VMEM((8, 8, 128), F32),
            pltpu.VMEM((8, 8, 128), F32),
            pltpu.VMEM((8, 64, 128), BF16),
            pltpu.VMEM((8, 32, 256), BF16),
            pltpu.SemaphoreType.DMA((7,)),
        ] + [pair_sems] * 8 + [pltpu.SemaphoreType.DMA((4, 2, 4))],
        compiler_params=pltpu.CompilerParams(
            collective_id=0, has_side_effects=True, vmem_limit_bytes=60 * 1024 * 1024
        ),
    )(
        field.T,
        quad_weight.reshape(1, 256),
        love_factor.reshape(8, 128),
        pair_table.reshape(1, 8),
        legendre.transpose(1, 0, 2).reshape(8200, 256),
        jnp.asarray(angle_constants()),
    )
    return grid.reshape(256, 256)[:, :LON_COLS].astype(F32)


def solution(mesh):
    placed = (P("lat", "lon"), P("lat"), P("lon", None, "lat"), P(), P("lon"))
    return jax.shard_map(
        per_device, mesh=mesh, in_specs=placed, out_specs=P("lat", "lon"), check_vma=False
    )
```

```python
import math

import jax
import jax.numpy as jnp
import ml_dtypes
import numpy as np
from jax import lax
from jax.experimental import pallas as pl
from jax.experimental.pallas import tpu as pltpu
from jax.sharding import PartitionSpec as P

F32 = jnp.float32
BF16 = jnp.bfloat16
TOTAL_LON = 8640
LON_COLS = 135
DEGREES = 1024
GROUPS = ((0, 4), (1, 7), (2, 6), (3, 5))
FAR_FIRST = (4, 3, 5, 2, 6, 1, 7)


def pair_orders():
    steps = 8 * np.arange(64)
    low = np.concatenate([steps + r for group in GROUPS for r in group])
    high = np.concatenate([steps + 7 - r for group in GROUPS for r in group])
    return low, high


def angle_constants():
    low, high = pair_orders()
    columns = np.arange(LON_COLS)
    made = np.zeros((8, 4, 2, 512, 256), ml_dtypes.bfloat16)
    for group in range(4):
        span = slice(128 * group, 128 * group + 128)
        orders = np.concatenate([low[span], DEGREES - 1 - high[span]])
        sign = np.ones((256, 1))
        if group:
            sign[64:128] = -1.0
            sign[192:256] = -1.0
        for q in range(8):
            turns = orders[:, None] * (LON_COLS * q + columns) % TOTAL_LON
            angle = turns * (2.0 * np.pi / TOTAL_LON)
            both = np.concatenate([np.cos(angle), np.sin(angle) * sign])
            head = both.astype(ml_dtypes.bfloat16)
            made[q, group, 0, :, :LON_COLS] = head
            made[q, group, 1, :, :LON_COLS] = (both - head.astype(np.float64)).astype(ml_dtypes.bfloat16)
    return made


def kernel(
    field_in, quad_in, love_in, pair_in, legendre, angles, out,
    field, quad, love, pair_own, pairs, leg, table, tail, last_rows, s1, r1, rp1, rp2, onehot, rhs, orders_all, s2, r2, s3, r3, four, s4, r4,
    factor, love_rows, blocks, s6, r6, r7, s8,
    local_sem, sem_pz, sem_pq, sem1, sem2, sem3, sem6, sem7, sem8, sem4,
):
    lon = lax.axis_index("lon")
    x = lax.axis_index("lat")
    z = lon // 8
    q = lon % 8

    def z_device(i):
        return {"lon": i * 8 + q}

    def q_device(i):
        return {"lon": z * 8 + i}

    def x_device(i):
        return {"lat": i}

    barrier = pltpu.get_barrier_semaphore()
    for d in FAR_FIRST:
        pl.semaphore_signal(barrier, inc=1, device_id=z_device((z + d) % 8))
    for d in FAR_FIRST:
        pl.semaphore_signal(barrier, inc=1, device_id=q_device((q + d) % 8))
    for d in range(1, 4):
        pl.semaphore_signal(barrier, inc=1, device_id=x_device((x + d) % 4))

    field_copy = pltpu.make_async_copy(field_in, field, local_sem.at[2])
    pair_copy = pltpu.make_async_copy(pair_in, pair_own, local_sem.at[3])
    love_copy = pltpu.make_async_copy(love_in, love, local_sem.at[4])
    quad_copy = pltpu.make_async_copy(quad_in, quad, local_sem.at[5])
    leg_copy = pltpu.make_async_copy(legendre, leg, local_sem.at[0])
    table_copy = pltpu.make_async_copy(angles.at[q], table, local_sem.at[1])
    for copy in (pair_copy, field_copy, love_copy, quad_copy, table_copy, leg_copy):
        copy.start()

    unsettled = []

    def send(distances, me, size, device, source, target, sems):
        copies = []
        for d in distances:
            to = (me + d) % size
            copy = pltpu.make_async_remote_copy(
                src_ref=source(to, d), dst_ref=target(d),
                send_sem=sems.at[0, d], recv_sem=sems.at[1, d],
                device_id=device(to),
            )
            copy.start()
            copies.append(copy)
        unsettled.extend(copies)
        return copies

    def settle(keep=0):
        while len(unsettled) > keep:
            unsettled.pop(0).wait_send()

    def arrive(copies):
        for copy in copies:
            copy.wait_recv()

    def arrived(target, sems, d):
        pltpu.make_async_remote_copy(
            src_ref=target, dst_ref=target, send_sem=sems.at[0, d], recv_sem=sems.at[1, d],
            device_id=z_device((z + d) % 8),
        ).wait_recv()

    lane = lax.broadcasted_iota(jnp.int32, (1, 128), 1)
    quarter = lane // 32
    step_in_tile = lane // 8

    last_rows[...] = jnp.zeros_like(last_rows)
    pair_copy.wait()
    spread = jnp.concatenate([pair_own[...].astype(F32), jnp.zeros((1, 120), F32)], axis=1)
    for shift in (8, 16, 32, 64):
        spread = spread + pltpu.roll(spread, shift, 1)
    pairs[...] = jnp.broadcast_to(spread, (8, 128))
    field_copy.wait()
    last_rows[0:15, :] = field[120:135, :]
    for h in range(2):
        cols = slice(128 * h, 128 * h + 128)
        runs = [field[40 * c:40 * c + 40, cols] for c in range(3)] + [last_rows[:, cols]]
        for g in range(4):
            packed = pltpu.roll(runs[0], (32 * (0 - g)) % 128, 1) if g else runs[0]
            for c in range(1, 4):
                moved = pltpu.roll(runs[c], (32 * (c - g)) % 128, 1) if c != g else runs[c]
                packed = jnp.where(quarter == c, moved, packed)
            s1[4 * h + g] = packed

    pl.semaphore_wait(barrier, 17)
    copies_pq = send(FAR_FIRST, q, 8, q_device, lambda to, d: pairs, lambda d: rp1.at[q], sem_pq)
    copies1 = send(FAR_FIRST, z, 8, z_device, lambda to, d: s1.at[to], lambda d: r1.at[z], sem1)
    r1[z] = s1[z]
    rp1[q] = pairs[...]

    tile_row = lax.broadcasted_iota(jnp.int32, (8, 128), 0)
    rhs[...] = jnp.zeros_like(rhs)
    s4[...] = jnp.zeros_like(s4)
    tail[...] = jnp.zeros_like(tail)
    love_rows[...] = jnp.zeros_like(love_rows)
    arrive(copies_pq)
    gathered = rp1[0]
    for i in range(1, 8):
        gathered = jnp.where(tile_row == i, rp1[i], gathered)
    rp2[z] = gathered
    send(FAR_FIRST, z, 8, z_device, lambda to, d: rp2.at[z], lambda d: rp2.at[z], sem_pz)

    pair_lane = pairs[0:1, :]
    love_copy.wait()
    love_rows[1:9, :] = love[...]
    love16 = love_rows[...]
    lane_row = lax.broadcasted_iota(jnp.int32, (128, 128), 0).astype(F32)
    step_f = step_in_tile.astype(F32)

    def shifted_love(start):
        whole = jnp.floor(start * (1.0 / 128.0))
        picked = jnp.where(lane_row == start - 128.0 * whole, 1.0, 0.0).astype(F32)
        rows = jnp.dot(love16, picked, preferred_element_type=F32, precision=lax.Precision.HIGHEST)
        for bit in (4, 2, 1):
            half = jnp.floor(whole * (1.0 / bit))
            odd = half - 2.0 * jnp.floor(half * 0.5)
            rows = jnp.where(odd > 0.5, pltpu.roll(rows, 16 - bit, 0), rows)
        return rows

    def column_ids(t0):
        return 128 * tile_row + (16 * t0 + step_in_tile)

    pair_int = pair_lane.astype(jnp.int32)
    for t0 in range(8):
        low_love = shifted_love(step_f + (pair_lane + (16.0 * t0 + 128.0)))
        high_love = shifted_love(step_f + (16.0 * t0 + 127.0))
        is_low = column_ids(t0) < DEGREES - pair_int
        factor[pl.ds(t0, 8, stride=8), :] = jnp.where(is_low, low_love[0:8], high_love[0:8])
        if t0 == 0:
            factor[64:72, :] = high_love[8:16]

    place = lax.broadcasted_iota(jnp.int32, (1, 1024), 1)
    group = place % 512 // 128
    other = jnp.where(group == 0, 4, 8 - group)
    residue = jnp.where(place % 128 < 64, group, other)
    wanted = (8 * (place % 64) + jnp.where(place < 512, residue, 7 - residue)).astype(F32)
    diagonal = lax.broadcasted_iota(jnp.int32, (16, 128), 0) % 8 == lane

    table_copy.wait()
    arrive(copies1)
    f = [r1[i] for i in range(8)]
    a = [f[i] - f[i + 4] for i in range(4)]
    b = [f[i] + f[i + 4] for i in range(4)]
    root = math.sqrt(0.5)
    a13m = root * (a[1] - a[3])
    a13p = root * (a[1] + a[3])
    parts = (
        (b[0] + b[1] + b[2] + b[3], b[0] - b[1] + b[2] - b[3]),
        (a[0] + a13m, -a[2] - a13p),
        (b[0] - b[2], b[3] - b[1]),
        (a[0] - a13m, a[2] - a13p),
    )

    def turned(value, by):
        return pltpu.roll(value, by % 128, value.ndim - 1) if by % 128 else value

    for g in range(4):
        re, im = parts[g]
        for c in range(4):
            rhs[g, 40 * c:40 * c + 40, :] = jnp.where(
                quarter < 2,
                jnp.where(quarter == 0, turned(re, -32 * c), turned(im, 32 - 32 * c)),
                jnp.where(quarter == 2, turned(re, 64 - 32 * c), turned(im, 96 - 32 * c)),
            )
    for g in range(4):
        value = rhs[g]
        head = value.astype(BF16).astype(F32)
        both = jnp.where(lane < 64, head, value - head).astype(BF16)
        first = jnp.dot(table[g, 0], both, preferred_element_type=F32)
        second = jnp.dot(table[g, 1], both, preferred_element_type=F32)
        total = first + turned(first, 64) + second
        d1, d2 = total[0:256], total[256:512]
        if g:
            spectrum = d1 + jnp.where(quarter == 0, turned(d2, 96), -turned(d2, 32))
            flipped = jnp.where(quarter == 1, -spectrum, spectrum)
            rows = (spectrum[0:64], flipped[64:128], spectrum[128:192], flipped[192:256])
        else:
            plain = jnp.where(quarter == 0, d1, -turned(d2, 32))
            other = jnp.where(quarter == 0, turned(d1, 96), -d2)
            rows = (plain[0:64], other[64:128], plain[128:192], other[192:256])
        for half in range(2):
            at = 128 * g + 64 * half
            orders_all[at:at + 64, :] = jnp.where(lane < 64, rows[half], 0.0)
            orders_all[512 + at:512 + at + 64, :] = jnp.where(lane < 64, 0.0, turned(rows[2 + half], 64))
    value = orders_all[...]
    head = value.astype(BF16)
    rest = (value - head.astype(F32)).astype(BF16)

    odd = z % 2
    near_other = 2 + 4 * odd
    far_other = 6 - 4 * odd

    def plane_pair(half, i):
        return (z // 2 + odd + 3 + 2 * half + i) % 4

    copies2 = []
    for half in range(2):
        for d in ((1, 7, near_other), (3, 4, 5, far_other))[half]:
            arrived(rp2.at[z], sem_pz, d)
        columns = []
        for i in range(2):
            first, second = rp2[2 * plane_pair(half, i)], rp2[2 * plane_pair(half, i) + 1]
            for to in range(8):
                both = jnp.concatenate([
                    jnp.broadcast_to(first[to:to + 1], (8, 128)), jnp.broadcast_to(second[to:to + 1], (8, 128))
                ], axis=0)
                columns.append(jnp.sum(jnp.where(diagonal, both, 0.0), axis=1, keepdims=True))
        for i in range(2):
            for to in range(8):
                at = pl.multiple_of(64 * to + 16 * plane_pair(half, i), 16)
                onehot[pl.ds(at, 16), :] = jnp.where(columns[8 * i + to] == wanted, 1.0, 0.0).astype(BF16)
        rows = jnp.concatenate([
            onehot[pl.ds(pl.multiple_of((q + d) % 8 * 64 + 16 * plane_pair(half, i), 16), 16), :]
            for d in range(8) for i in range(2)
        ], axis=0)
        in_slots = jnp.dot(rows, head, preferred_element_type=F32) + jnp.dot(rows, rest, preferred_element_type=F32)
        s2[half] = in_slots.reshape(8, 32, 128)
        copies2.append(send(
            FAR_FIRST, q, 8, q_device, lambda to, d: s2.at[half, d], lambda d: r2.at[half, d], sem2.at[half]
        ))
    settle(14)

    for half in range(2):
        arrive(copies2[half])
        total = s2[half, 0]
        for d in range(1, 8):
            total = total + r2[half, d]
        for i in range(2):
            for plane in range(2):
                s3[2 * plane_pair(half, i) + plane] = total[16 * i + 8 * plane:16 * i + 8 * plane + 8]
        send(
            ((7, 1, far_other), (4, 3, 5, near_other))[half], z, 8, z_device,
            lambda to, d: s3.at[to], lambda d: r3.at[z], sem3,
        )
    r3[z] = s3[z]

    quad_copy.wait()
    leg_copy.wait()
    tail[0:8, :] = leg[8192:8200, :].astype(F32)
    settle(7)
    for d in range(1, 8):
        arrived(r3.at[z], sem3, d)
    for r in range(2):
        for o in range(2):
            j = 2 * o + r
            for h in range(2):
                cols = slice(128 * h, 128 * h + 128)
                tile = turned(r3[4 * h], -32 * j)
                for g in range(1, 4):
                    tile = jnp.where(quarter == g, turned(r3[4 * h + g], 32 * (g - j)), tile)
                at = 16 * r + 8 * o
                four[at:at + 8, cols] = tile / float(TOTAL_LON) * quad[0:1, cols]
    fourier = four[...].astype(BF16)

    own_slot = lane % 8 == tile_row
    low_limit = DEGREES - pair_int - step_in_tile
    tail_rows = tail[...].astype(BF16)

    def analysed(piece, is_low, r):
        if is_low is None:
            picked = piece[16 * r + 8:16 * r + 16]
        else:
            picked = jnp.where(is_low, piece[16 * r:16 * r + 8], piece[16 * r + 8:16 * r + 16])
        return jnp.sum(jnp.where(own_slot, picked, 0.0), axis=0, keepdims=True)

    product = lax.dot_general(fourier, tail_rows, (((1,), (1,)), ((), ())), preferred_element_type=F32)
    for r in range(2):
        s4[0, 32 + r:33 + r, :] = analysed(product, None, r)
    copies4 = []
    for chunk in range(4):
        product = lax.dot_general(
            fourier, leg[2048 * chunk:2048 * chunk + 2048, :], (((1,), (1,)), ((), ())), preferred_element_type=F32
        )
        for row in range(16):
            is_low = jnp.broadcast_to(16 * (16 * chunk + row) < low_limit, (8, 128))
            for r in range(2):
                s4[chunk, 16 * r + row:16 * r + row + 1, :] = analysed(
                    product[:, 128 * row:128 * row + 128], is_low, r
                )
        size = 32 if chunk else 40
        copies4.append(send(
            (2, 1, 3), x, 4, x_device,
            lambda to, d: s4.at[chunk, pl.ds(0, size)], lambda d: r4.at[d, chunk, pl.ds(0, size)], sem4.at[chunk],
        ))

    settle(12)
    profile = jnp.zeros((32, 256), F32)
    for chunk in range(4):
        arrive(copies4[chunk])
        total = s4[chunk] + r4[1, chunk] + r4[2, chunk] + r4[3, chunk]
        scale = factor[16 * chunk:16 * chunk + 16, :]
        spectral = jnp.concatenate([total[0:16] * scale, total[16:32] * scale], axis=0).astype(BF16).astype(F32)
        for row in range(16):
            is_low = jnp.broadcast_to(16 * (16 * chunk + row) < low_limit, (8, 128))
            pieces = []
            for r in range(2):
                line = jnp.broadcast_to(spectral[16 * r + row:16 * r + row + 1], (8, 128))
                line = jnp.where(own_slot, line, 0.0)
                pieces += [jnp.where(is_low, line, 0.0), jnp.where(is_low, 0.0, line)]
            blocks[chunk, :, 128 * row:128 * row + 128] = jnp.concatenate(pieces, axis=0).astype(BF16)
        profile = profile + jnp.dot(
            blocks[chunk], leg[2048 * chunk:2048 * chunk + 2048, :], preferred_element_type=F32
        )
        if chunk == 0:
            last = (total[32:40] * factor[64:65, :]).astype(BF16).astype(F32)
            pieces = []
            for r in range(2):
                line = jnp.where(own_slot, jnp.broadcast_to(last[r:r + 1], (8, 128)), 0.0)
                pieces += [jnp.zeros((8, 128), F32), line]
            profile = profile + jnp.dot(
                jnp.concatenate(pieces, axis=0).astype(BF16), tail_rows, preferred_element_type=F32
            )
    profile = profile.astype(BF16).astype(F32)

    for h in range(2):
        for g in range(4):
            tile = turned(profile[0:8, 128 * h:128 * h + 128], -32 * g)
            for j in range(1, 4):
                at = 16 * (j % 2) + 8 * (j // 2)
                tile = jnp.where(
                    quarter == j, turned(profile[at:at + 8, 128 * h:128 * h + 128], 32 * (j - g)), tile
                )
            s6[4 * h + g] = tile
    copies6 = send(FAR_FIRST, z, 8, z_device, lambda to, d: s6.at[to], lambda d: r6.at[z], sem6)
    r6[z] = s6[z]
    settle(7)
    arrive(copies6)

    r7[q] = r6[...].reshape(64, 128).astype(BF16)
    copies7 = send(FAR_FIRST, q, 8, q_device, lambda to, d: r7.at[q], lambda d: r7.at[q], sem7)
    settle(7)
    arrive(copies7)
    natural = lax.dot_general(
        r7[...].reshape(512, 128), onehot[...], (((0,), (0,)), ((), ())), preferred_element_type=F32
    )
    wide_lane = lax.broadcasted_iota(jnp.int32, (1, 256), 1)
    second_half = wide_lane % 128 >= 64
    waves = []
    for g in range(4):
        low = slice(128 * g, 128 * g + 128)
        high = slice(512 + 128 * g, 640 + 128 * g)
        re = jnp.concatenate([natural[0:32, low], natural[64:96, high]], axis=1)
        im = jnp.concatenate([natural[32:64, low], natural[96:128, high]], axis=1)
        if g:
            left = jnp.concatenate([re, jnp.where(second_half, -im, im)], axis=0)
        else:
            re = jnp.where(wide_lane == 0, 0.5 * re, re)
            im = jnp.where(wide_lane == 0, 0.5 * im, im)
            left = jnp.concatenate([
                jnp.where(second_half, 0.0, re), jnp.where(second_half, 0.0, im),
                jnp.where(second_half, re, 0.0), jnp.where(second_half, im, 0.0),
            ], axis=0)
        left = left.astype(BF16)
        by_cos = jnp.dot(left, table[g, 0, 0:256], preferred_element_type=F32) + jnp.dot(
            left, table[g, 1, 0:256], preferred_element_type=F32
        )
        by_sin = jnp.dot(left, table[g, 0, 256:512], preferred_element_type=F32) + jnp.dot(
            left, table[g, 1, 256:512], preferred_element_type=F32
        )
        if g:
            waves.append((by_cos[0:32] - by_sin[32:64], by_sin[0:32] + by_cos[32:64]))
        else:
            waves.append((by_cos[0:32] - by_sin[32:64], by_cos[64:96] - by_sin[96:128]))
    (w0, w4), (re1, im1), (re2, im2), (re3, im3) = waves
    even0, even1 = w0 + w4, w0 - w4
    re_sum, re_dif = re1 + re3, root * (re1 - re3)
    im_dif, im_sum = im1 - im3, root * (im1 + im3)
    b0, b1, b2, b3 = even0 + re2, even1 - im2, even0 - re2, even1 + im2
    a0, a1, a2, a3 = re_sum, re_dif - im_sum, -im_dif, -re_dif - im_sum
    for i, value in enumerate((b0 + a0, b1 + a1, b2 + a2, b3 + a3, b0 - a0, b1 - a1, b2 - a2, b3 - a3)):
        s8[i] = (2.0 * value).astype(BF16)

    copies8 = send(FAR_FIRST, z, 8, z_device, lambda to, d: s8.at[to], lambda d: out.at[z], sem8)
    own_copy = pltpu.make_async_copy(s8.at[z], out.at[z], local_sem.at[6])
    own_copy.start()
    settle(7)
    arrive(copies8)
    own_copy.wait()
    settle()


def per_device(field, quad_weight, legendre, love_factor, pair_table):
    anywhere = pl.BlockSpec(memory_space=pl.ANY)
    pair_sems = pltpu.SemaphoreType.DMA((2, 8))
    grid = pl.pallas_call(
        kernel,
        out_shape=jax.ShapeDtypeStruct((8, 32, 256), BF16),
        in_specs=[anywhere] * 6,
        out_specs=anywhere,
        scratch_shapes=[
            pltpu.VMEM((LON_COLS, 256), F32),
            pltpu.VMEM((1, 256), F32),
            pltpu.VMEM((8, 128), F32),
            pltpu.VMEM((1, 8), jnp.int32),
            pltpu.VMEM((8, 128), F32),
            pltpu.VMEM((8200, 256), BF16),
            pltpu.VMEM((4, 2, 512, 256), BF16),
            pltpu.VMEM((128, 256), F32),
            pltpu.VMEM((40, 256), F32),
            pltpu.VMEM((8, 40, 128), F32),
            pltpu.VMEM((8, 40, 128), F32),
            pltpu.VMEM((8, 8, 128), F32),
            pltpu.VMEM((8, 8, 128), F32),
            pltpu.VMEM((512, 1024), BF16),
            pltpu.VMEM((4, 256, 128), F32),
            pltpu.VMEM((1024, 128), F32),
            pltpu.VMEM((2, 8, 32, 128), F32),
            pltpu.VMEM((2, 8, 32, 128), F32),
            pltpu.VMEM((8, 8, 128), F32),
            pltpu.VMEM((8, 8, 128), F32),
            pltpu.VMEM((32, 256), F32),
            pltpu.VMEM((4, 40, 128), F32),
            pltpu.VMEM((4, 4, 40, 128), F32),
            pltpu.VMEM((72, 128), F32),
            pltpu.VMEM((16, 128), F32),
            pltpu.VMEM((4, 32, 2048), BF16),
            pltpu.VMEM((8, 8, 128), F32),
            pltpu.VMEM((8, 8, 128), F32),
            pltpu.VMEM((8, 64, 128), BF16),
            pltpu.VMEM((8, 32, 256), BF16),
            pltpu.SemaphoreType.DMA((7,)),
        ] + [pair_sems] * 3 + [pltpu.SemaphoreType.DMA((2, 2, 8))] + [pair_sems] * 4 + [pltpu.SemaphoreType.DMA((4, 2, 4))],
        compiler_params=pltpu.CompilerParams(
            collective_id=0, has_side_effects=True, vmem_limit_bytes=60 * 1024 * 1024
        ),
    )(
        field.T,
        quad_weight.reshape(1, 256),
        love_factor.reshape(8, 128),
        pair_table.reshape(1, 8),
        legendre.transpose(1, 0, 2).reshape(8200, 256),
        jnp.asarray(angle_constants()),
    )
    return grid.reshape(256, 256)[:, :LON_COLS].astype(F32)


def solution(mesh):
    placed = (P("lat", "lon"), P("lat"), P("lon", None, "lat"), P(), P("lon"))
    return jax.shard_map(
        per_device, mesh=mesh, in_specs=placed, out_specs=P("lat", "lon"), check_vma=False
    )
```

```python
import math

import jax
import jax.numpy as jnp
import ml_dtypes
import numpy as np
from jax import lax
from jax.experimental import pallas as pl
from jax.experimental.pallas import tpu as pltpu
from jax.sharding import PartitionSpec as P

F32 = jnp.float32
BF16 = jnp.bfloat16
TOTAL_LON = 8640
LON_COLS = 135
DEGREES = 1024
GROUPS = ((0, 4), (1, 7), (2, 6), (3, 5))
FAR_FIRST = (4, 3, 5, 2, 6, 1, 7)


def pair_orders():
    steps = 8 * np.arange(64)
    low = np.concatenate([steps + r for group in GROUPS for r in group])
    high = np.concatenate([steps + 7 - r for group in GROUPS for r in group])
    return low, high


def angle_constants():
    low, high = pair_orders()
    columns = np.arange(LON_COLS)
    made = np.zeros((8, 4, 2, 512, 256), ml_dtypes.bfloat16)
    for group in range(4):
        span = slice(128 * group, 128 * group + 128)
        orders = np.concatenate([low[span], DEGREES - 1 - high[span]])
        sign = np.ones((256, 1))
        if group:
            sign[64:128] = -1.0
            sign[192:256] = -1.0
        for q in range(8):
            turns = orders[:, None] * (LON_COLS * q + columns) % TOTAL_LON
            angle = turns * (2.0 * np.pi / TOTAL_LON)
            both = np.concatenate([np.cos(angle), np.sin(angle) * sign])
            head = both.astype(ml_dtypes.bfloat16)
            made[q, group, 0, :, :LON_COLS] = head
            made[q, group, 1, :, :LON_COLS] = (both - head.astype(np.float64)).astype(ml_dtypes.bfloat16)
    return made


def kernel(
    field_in, quad_in, love_in, pair_in, legendre, angles, out,
    field, quad, love, pair_own, pairs, leg, table, tail, last_rows, s1, r1, rp1, rp2, onehot, rhs, orders_all, s2, r2, s3, r3, four, s4, r4,
    factor, love_rows, spectral, blocks, s6, r6, r7, s8,
    local_sem, sem_pz, sem_pq, sem1, sem2, sem3, sem6, sem7, sem8, sem4,
):
    lon = lax.axis_index("lon")
    x = lax.axis_index("lat")
    z = lon // 8
    q = lon % 8

    def z_device(i):
        return {"lon": i * 8 + q}

    y = q // 2
    core = q % 2

    def zy_device(i, j):
        return {"lon": i * 8 + 2 * j + core}

    other_core = {"lon": z * 8 + 2 * y + 1 - core}

    def q_device(i):
        return {"lon": z * 8 + i}

    def x_device(i):
        return {"lat": i}

    barrier = pltpu.get_barrier_semaphore()
    for d in FAR_FIRST:
        pl.semaphore_signal(barrier, inc=1, device_id=z_device((z + d) % 8))
    for d in FAR_FIRST:
        pl.semaphore_signal(barrier, inc=1, device_id=q_device((q + d) % 8))
    for d in range(1, 4):
        pl.semaphore_signal(barrier, inc=1, device_id=x_device((x + d) % 4))

    field_copy = pltpu.make_async_copy(field_in, field, local_sem.at[2])
    pair_copy = pltpu.make_async_copy(pair_in, pair_own, local_sem.at[3])
    love_copy = pltpu.make_async_copy(love_in, love, local_sem.at[4])
    quad_copy = pltpu.make_async_copy(quad_in, quad, local_sem.at[5])
    leg_copy = pltpu.make_async_copy(legendre, leg, local_sem.at[0])
    table_copy = pltpu.make_async_copy(angles.at[q], table, local_sem.at[1])
    for copy in (pair_copy, field_copy, love_copy, quad_copy, table_copy, leg_copy):
        copy.start()

    unsettled = []

    def send_one(source, target, send_sem, recv_sem, device):
        copy = pltpu.make_async_remote_copy(
            src_ref=source, dst_ref=target, send_sem=send_sem, recv_sem=recv_sem, device_id=device
        )
        copy.start()
        unsettled.append(copy)
        return copy

    def arrived_zy(target, sems, dz, dy):
        pltpu.make_async_remote_copy(
            src_ref=target, dst_ref=target, send_sem=sems.at[0, dz, dy], recv_sem=sems.at[1, dz, dy],
            device_id=zy_device((z + 1) % 8, y),
        ).wait_recv()

    def send(distances, me, size, device, source, target, sems):
        copies = []
        for d in distances:
            to = (me + d) % size
            copy = pltpu.make_async_remote_copy(
                src_ref=source(to, d), dst_ref=target(d),
                send_sem=sems.at[0, d], recv_sem=sems.at[1, d],
                device_id=device(to),
            )
            copy.start()
            copies.append(copy)
        unsettled.extend(copies)
        return copies

    def settle(keep=0):
        while len(unsettled) > keep:
            unsettled.pop(0).wait_send()

    def arrive(copies):
        for copy in copies:
            copy.wait_recv()

    def arrived(target, sems, d):
        pltpu.make_async_remote_copy(
            src_ref=target, dst_ref=target, send_sem=sems.at[0, d], recv_sem=sems.at[1, d],
            device_id=z_device((z + d) % 8),
        ).wait_recv()

    lane = lax.broadcasted_iota(jnp.int32, (1, 128), 1)
    quarter = lane // 32
    step_in_tile = lane // 8

    last_rows[...] = jnp.zeros_like(last_rows)
    pair_copy.wait()
    spread = jnp.concatenate([pair_own[...].astype(F32), jnp.zeros((1, 120), F32)], axis=1)
    for shift in (8, 16, 32, 64):
        spread = spread + pltpu.roll(spread, shift, 1)
    pairs[...] = jnp.broadcast_to(spread, (8, 128))
    field_copy.wait()
    last_rows[0:15, :] = field[120:135, :]
    for h in range(2):
        cols = slice(128 * h, 128 * h + 128)
        runs = [field[40 * c:40 * c + 40, cols] for c in range(3)] + [last_rows[:, cols]]
        for g in range(4):
            packed = pltpu.roll(runs[0], (32 * (0 - g)) % 128, 1) if g else runs[0]
            for c in range(1, 4):
                moved = pltpu.roll(runs[c], (32 * (c - g)) % 128, 1) if c != g else runs[c]
                packed = jnp.where(quarter == c, moved, packed)
            s1[4 * h + g] = packed

    pl.semaphore_wait(barrier, 17)
    copies_pq = send(FAR_FIRST, q, 8, q_device, lambda to, d: pairs, lambda d: rp1.at[q], sem_pq)
    copies1 = send(FAR_FIRST, z, 8, z_device, lambda to, d: s1.at[to], lambda d: r1.at[z], sem1)
    r1[z] = s1[z]
    rp1[q] = pairs[...]

    tile_row = lax.broadcasted_iota(jnp.int32, (8, 128), 0)
    rhs[...] = jnp.zeros_like(rhs)
    s4[...] = jnp.zeros_like(s4)
    tail[...] = jnp.zeros_like(tail)
    love_rows[...] = jnp.zeros_like(love_rows)
    arrive(copies_pq)
    gathered = rp1[0]
    for i in range(1, 8):
        gathered = jnp.where(tile_row == i, rp1[i], gathered)
    rp2[z] = gathered
    send(FAR_FIRST, z, 8, z_device, lambda to, d: rp2.at[z], lambda d: rp2.at[z], sem_pz)

    pair_lane = pairs[0:1, :]
    love_copy.wait()
    love_rows[1:9, :] = love[...]
    love16 = love_rows[...]
    lane_row = lax.broadcasted_iota(jnp.int32, (128, 128), 0).astype(F32)
    step_f = step_in_tile.astype(F32)

    def shifted_love(start):
        whole = jnp.floor(start * (1.0 / 128.0))
        picked = jnp.where(lane_row == start - 128.0 * whole, 1.0, 0.0).astype(F32)
        rows = jnp.dot(love16, picked, preferred_element_type=F32, precision=lax.Precision.HIGHEST)
        for bit in (4, 2, 1):
            half = jnp.floor(whole * (1.0 / bit))
            odd = half - 2.0 * jnp.floor(half * 0.5)
            rows = jnp.where(odd > 0.5, pltpu.roll(rows, 16 - bit, 0), rows)
        return rows

    def column_ids(t0):
        return 128 * tile_row + (16 * t0 + step_in_tile)

    pair_int = pair_lane.astype(jnp.int32)
    for t0 in range(8):
        low_love = shifted_love(step_f + (pair_lane + (16.0 * t0 + 128.0)))
        high_love = shifted_love(step_f + (16.0 * t0 + 127.0))
        is_low = column_ids(t0) < DEGREES - pair_int
        factor[pl.ds(t0, 8, stride=8), :] = jnp.where(is_low, low_love[0:8], high_love[0:8])
        if t0 == 0:
            factor[64:72, :] = high_love[8:16]

    place = lax.broadcasted_iota(jnp.int32, (1, 1024), 1)
    group = place % 512 // 128
    other = jnp.where(group == 0, 4, 8 - group)
    residue = jnp.where(place % 128 < 64, group, other)
    wanted = (8 * (place % 64) + jnp.where(place < 512, residue, 7 - residue)).astype(F32)
    diagonal = lax.broadcasted_iota(jnp.int32, (16, 128), 0) % 8 == lane

    table_copy.wait()
    arrive(copies1)
    f = [r1[i] for i in range(8)]
    a = [f[i] - f[i + 4] for i in range(4)]
    b = [f[i] + f[i + 4] for i in range(4)]
    root = math.sqrt(0.5)
    a13m = root * (a[1] - a[3])
    a13p = root * (a[1] + a[3])
    parts = (
        (b[0] + b[1] + b[2] + b[3], b[0] - b[1] + b[2] - b[3]),
        (a[0] + a13m, -a[2] - a13p),
        (b[0] - b[2], b[3] - b[1]),
        (a[0] - a13m, a[2] - a13p),
    )

    def turned(value, by):
        return pltpu.roll(value, by % 128, value.ndim - 1) if by % 128 else value

    for g in range(4):
        re, im = parts[g]
        for c in range(4):
            rhs[g, 40 * c:40 * c + 40, :] = jnp.where(
                quarter < 2,
                jnp.where(quarter == 0, turned(re, -32 * c), turned(im, 32 - 32 * c)),
                jnp.where(quarter == 2, turned(re, 64 - 32 * c), turned(im, 96 - 32 * c)),
            )
    for g in range(4):
        value = rhs[g]
        head = value.astype(BF16).astype(F32)
        both = jnp.where(lane < 64, head, value - head).astype(BF16)
        first = jnp.dot(table[g, 0], both, preferred_element_type=F32)
        second = jnp.dot(table[g, 1], both, preferred_element_type=F32)
        total = first + turned(first, 64) + second
        d1, d2 = total[0:256], total[256:512]
        if g:
            spectrum = d1 + jnp.where(quarter == 0, turned(d2, 96), -turned(d2, 32))
            flipped = jnp.where(quarter == 1, -spectrum, spectrum)
            rows = (spectrum[0:64], flipped[64:128], spectrum[128:192], flipped[192:256])
        else:
            plain = jnp.where(quarter == 0, d1, -turned(d2, 32))
            other = jnp.where(quarter == 0, turned(d1, 96), -d2)
            rows = (plain[0:64], other[64:128], plain[128:192], other[192:256])
        for half in range(2):
            at = 128 * g + 64 * half
            for o in range(2):
                value = rows[2 * o + half]
                head = value.astype(BF16).astype(F32)
                orders_all[o, at:at + 64, :] = jnp.where(lane < 64, head, turned(value - head, 64)).astype(BF16)

    odd = z % 2
    near_other = 2 + 4 * odd
    far_other = 6 - 4 * odd

    def plane_pair(half, i):
        return (z // 2 + odd + 3 + 2 * half + i) % 4

    copies2 = []
    for half in range(2):
        for d in ((1, 7, near_other), (3, 4, 5, far_other))[half]:
            arrived(rp2.at[z], sem_pz, d)
        columns = []
        for i in range(2):
            first, second = rp2[2 * plane_pair(half, i)], rp2[2 * plane_pair(half, i) + 1]
            for to in range(8):
                both = jnp.concatenate([
                    jnp.broadcast_to(first[to:to + 1], (8, 128)), jnp.broadcast_to(second[to:to + 1], (8, 128))
                ], axis=0)
                columns.append(jnp.sum(jnp.where(diagonal, both, 0.0), axis=1, keepdims=True))
        for i in range(2):
            for to in range(8):
                at = pl.multiple_of(64 * to + 16 * plane_pair(half, i), 16)
                onehot[pl.ds(at, 16), :] = jnp.where(columns[8 * i + to] == wanted, 1.0, 0.0).astype(BF16)
        rows = jnp.concatenate([
            onehot[pl.ds(pl.multiple_of(
                64 * (2 * ((y + dy) % 4) + (core + e) % 2) + 16 * plane_pair(half, i), 16
            ), 16), :]
            for e in range(2) for dy in range(4) for i in range(2)
        ], axis=0)
        low_part = jnp.dot(rows[:, 0:512], orders_all[0], preferred_element_type=F32)
        high_part = jnp.dot(rows[:, 512:1024], orders_all[1], preferred_element_type=F32)
        in_slots = jnp.where(lane < 64, low_part + turned(low_part, 64), high_part + turned(high_part, 64))
        s2[half] = in_slots.reshape(2, 128, 128)
        copies2.append(send_one(
            s2.at[half, 1], r2.at[half], sem2.at[0, half], sem2.at[1, half], other_core
        ))
    settle(2)

    for half in range(2):
        copies2[half].wait_recv()
        total = s2[half, 0] + r2[half]
        for dy in range(4):
            for i in range(2):
                for plane in range(2):
                    at = 32 * dy + 16 * i + 8 * plane
                    s3[dy, 2 * plane_pair(half, i) + plane] = total[at:at + 8]
        for dz in ((far_other, 1, 7, 0), (4, 3, 5, near_other))[half]:
            for dy in (2, 1, 3, 0):
                if isinstance(dz, int) and dz == 0 and dy == 0:
                    continue
                send_one(
                    s3.at[dy, (z + dz) % 8], r3.at[y, z], sem3.at[0, dz, dy], sem3.at[1, dz, dy],
                    zy_device((z + dz) % 8, (y + dy) % 4),
                )
    r3[y, z] = s3[0, z]

    quad_copy.wait()
    leg_copy.wait()
    tail[0:8, :] = leg[8192:8200, :].astype(F32)
    settle(31)
    for dz in range(8):
        for dy in range(4):
            if dz or dy:
                arrived_zy(r3.at[y, z], sem3, dz, dy)
    own_sums = [r3[0, i] + r3[1, i] + r3[2, i] + r3[3, i] for i in range(8)]
    for r in range(2):
        for o in range(2):
            j = 2 * o + r
            for h in range(2):
                cols = slice(128 * h, 128 * h + 128)
                tile = turned(own_sums[4 * h], -32 * j)
                for g in range(1, 4):
                    tile = jnp.where(quarter == g, turned(own_sums[4 * h + g], 32 * (g - j)), tile)
                at = 16 * r + 8 * o
                four[at:at + 8, cols] = tile / float(TOTAL_LON) * quad[0:1, cols]
    fourier = four[...].astype(BF16)

    own_slot = lane % 8 == tile_row
    low_limit = DEGREES - pair_int - step_in_tile
    tail_rows = tail[...].astype(BF16)

    def analysed(piece, is_low, r):
        if is_low is None:
            picked = piece[16 * r + 8:16 * r + 16]
        else:
            picked = jnp.where(is_low, piece[16 * r:16 * r + 8], piece[16 * r + 8:16 * r + 16])
        return jnp.sum(jnp.where(own_slot, picked, 0.0), axis=0, keepdims=True)

    product = lax.dot_general(fourier, tail_rows, (((1,), (1,)), ((), ())), preferred_element_type=F32)
    for r in range(2):
        s4[0, 32 + r:33 + r, :] = analysed(product, None, r)
    copies4 = []
    for chunk in range(4):
        product = lax.dot_general(
            fourier, leg[2048 * chunk:2048 * chunk + 2048, :], (((1,), (1,)), ((), ())), preferred_element_type=F32
        )
        for row in range(16):
            is_low = jnp.broadcast_to(16 * (16 * chunk + row) < low_limit, (8, 128))
            for r in range(2):
                s4[chunk, 16 * r + row:16 * r + row + 1, :] = analysed(
                    product[:, 128 * row:128 * row + 128], is_low, r
                )
        size = 32 if chunk else 40
        copies4.append(send(
            (2, 1, 3), x, 4, x_device,
            lambda to, d: s4.at[chunk, pl.ds(0, size)], lambda d: r4.at[d, chunk, pl.ds(0, size)], sem4.at[chunk],
        ))

    settle(12)
    profile = jnp.zeros((32, 256), F32)
    for chunk in range(4):
        arrive(copies4[chunk])
        total = s4[chunk] + r4[1, chunk] + r4[2, chunk] + r4[3, chunk]
        scale = factor[16 * chunk:16 * chunk + 16, :]
        spectral[chunk] = jnp.concatenate([total[0:16] * scale, total[16:32] * scale], axis=0).astype(BF16).astype(F32)
        for row in range(16):
            is_low = jnp.broadcast_to(16 * (16 * chunk + row) < low_limit, (8, 128))
            pieces = []
            for r in range(2):
                line = jnp.broadcast_to(spectral[chunk, 16 * r + row:16 * r + row + 1, :], (8, 128))
                line = jnp.where(own_slot, line, 0.0)
                pieces += [jnp.where(is_low, line, 0.0), jnp.where(is_low, 0.0, line)]
            blocks[chunk, :, 128 * row:128 * row + 128] = jnp.concatenate(pieces, axis=0).astype(BF16)
        profile = profile + jnp.dot(
            blocks[chunk], leg[2048 * chunk:2048 * chunk + 2048, :], preferred_element_type=F32
        )
        if chunk == 0:
            last = (total[32:40] * factor[64:65, :]).astype(BF16).astype(F32)
            pieces = []
            for r in range(2):
                line = jnp.where(own_slot, jnp.broadcast_to(last[r:r + 1], (8, 128)), 0.0)
                pieces += [jnp.zeros((8, 128), F32), line]
            profile = profile + jnp.dot(
                jnp.concatenate(pieces, axis=0).astype(BF16), tail_rows, preferred_element_type=F32
            )
    profile = profile.astype(BF16).astype(F32)

    for h in range(2):
        for g in range(4):
            tile = turned(profile[0:8, 128 * h:128 * h + 128], -32 * g)
            for j in range(1, 4):
                at = 16 * (j % 2) + 8 * (j // 2)
                tile = jnp.where(
                    quarter == j, turned(profile[at:at + 8, 128 * h:128 * h + 128], 32 * (j - g)), tile
                )
            s6[4 * h + g] = tile
    for dz in FAR_FIRST + (0,):
        for dy in (2, 1, 3, 0):
            if dz or dy:
                send_one(
                    s6.at[(z + dz) % 8], r6.at[y, z], sem6.at[0, dz, dy], sem6.at[1, dz, dy],
                    zy_device((z + dz) % 8, (y + dy) % 4),
                )
    r6[y, z] = s6[z]
    settle(31)

    copies7 = []
    for dy in (0, 1, 3, 2):
        for dz in range(8):
            if dz or dy:
                arrived_zy(r6.at[y, z], sem6, dz, dy)
        row = (y - dy + 4) % 4
        r7[row, core] = r6[row].reshape(64, 128).astype(BF16)
        copies7.append(send_one(
            r7.at[row, core], r7.at[row, core], sem7.at[0, dy], sem7.at[1, dy], other_core
        ))
    settle(4)
    arrive(copies7)
    natural = lax.dot_general(
        r7[...].reshape(512, 128), onehot[...], (((0,), (0,)), ((), ())), preferred_element_type=F32
    )
    wide_lane = lax.broadcasted_iota(jnp.int32, (1, 256), 1)
    second_half = wide_lane % 128 >= 64
    waves = []
    for g in range(4):
        low = slice(128 * g, 128 * g + 128)
        high = slice(512 + 128 * g, 640 + 128 * g)
        re = jnp.concatenate([natural[0:32, low], natural[64:96, high]], axis=1)
        im = jnp.concatenate([natural[32:64, low], natural[96:128, high]], axis=1)
        if g:
            left = jnp.concatenate([re, jnp.where(second_half, -im, im)], axis=0)
        else:
            re = jnp.where(wide_lane == 0, 0.5 * re, re)
            im = jnp.where(wide_lane == 0, 0.5 * im, im)
            left = jnp.concatenate([
                jnp.where(second_half, 0.0, re), jnp.where(second_half, 0.0, im),
                jnp.where(second_half, re, 0.0), jnp.where(second_half, im, 0.0),
            ], axis=0)
        left = left.astype(BF16)
        by_cos = jnp.dot(left, table[g, 0, 0:256], preferred_element_type=F32) + jnp.dot(
            left, table[g, 1, 0:256], preferred_element_type=F32
        )
        by_sin = jnp.dot(left, table[g, 0, 256:512], preferred_element_type=F32) + jnp.dot(
            left, table[g, 1, 256:512], preferred_element_type=F32
        )
        if g:
            waves.append((by_cos[0:32] - by_sin[32:64], by_sin[0:32] + by_cos[32:64]))
        else:
            waves.append((by_cos[0:32] - by_sin[32:64], by_cos[64:96] - by_sin[96:128]))
    (w0, w4), (re1, im1), (re2, im2), (re3, im3) = waves
    even0, even1 = w0 + w4, w0 - w4
    re_sum, re_dif = re1 + re3, root * (re1 - re3)
    im_dif, im_sum = im1 - im3, root * (im1 + im3)
    b0, b1, b2, b3 = even0 + re2, even1 - im2, even0 - re2, even1 + im2
    a0, a1, a2, a3 = re_sum, re_dif - im_sum, -im_dif, -re_dif - im_sum
    for i, value in enumerate((b0 + a0, b1 + a1, b2 + a2, b3 + a3, b0 - a0, b1 - a1, b2 - a2, b3 - a3)):
        s8[i] = (2.0 * value).astype(BF16)

    copies8 = send(FAR_FIRST, z, 8, z_device, lambda to, d: s8.at[to], lambda d: out.at[z], sem8)
    own_copy = pltpu.make_async_copy(s8.at[z], out.at[z], local_sem.at[6])
    own_copy.start()
    settle(7)
    arrive(copies8)
    own_copy.wait()
    settle()


def per_device(field, quad_weight, legendre, love_factor, pair_table):
    anywhere = pl.BlockSpec(memory_space=pl.ANY)
    pair_sems = pltpu.SemaphoreType.DMA((2, 8))
    plane_sems = pltpu.SemaphoreType.DMA((2, 8, 4))
    core_sems = pltpu.SemaphoreType.DMA((2, 4))
    grid = pl.pallas_call(
        kernel,
        out_shape=jax.ShapeDtypeStruct((8, 32, 256), BF16),
        in_specs=[anywhere] * 6,
        out_specs=anywhere,
        scratch_shapes=[
            pltpu.VMEM((LON_COLS, 256), F32),
            pltpu.VMEM((1, 256), F32),
            pltpu.VMEM((8, 128), F32),
            pltpu.VMEM((1, 8), jnp.int32),
            pltpu.VMEM((8, 128), F32),
            pltpu.VMEM((8200, 256), BF16),
            pltpu.VMEM((4, 2, 512, 256), BF16),
            pltpu.VMEM((128, 256), F32),
            pltpu.VMEM((40, 256), F32),
            pltpu.VMEM((8, 40, 128), F32),
            pltpu.VMEM((8, 40, 128), F32),
            pltpu.VMEM((8, 8, 128), F32),
            pltpu.VMEM((8, 8, 128), F32),
            pltpu.VMEM((512, 1024), BF16),
            pltpu.VMEM((4, 256, 128), F32),
            pltpu.VMEM((2, 512, 128), BF16),
            pltpu.VMEM((2, 2, 128, 128), F32),
            pltpu.VMEM((2, 128, 128), F32),
            pltpu.VMEM((4, 8, 8, 128), F32),
            pltpu.VMEM((4, 8, 8, 128), F32),
            pltpu.VMEM((32, 256), F32),
            pltpu.VMEM((4, 40, 128), F32),
            pltpu.VMEM((4, 4, 40, 128), F32),
            pltpu.VMEM((72, 128), F32),
            pltpu.VMEM((16, 128), F32),
            pltpu.VMEM((4, 32, 128), F32),
            pltpu.VMEM((4, 32, 2048), BF16),
            pltpu.VMEM((8, 8, 128), F32),
            pltpu.VMEM((4, 8, 8, 128), F32),
            pltpu.VMEM((4, 2, 64, 128), BF16),
            pltpu.VMEM((8, 32, 256), BF16),
            pltpu.SemaphoreType.DMA((7,)),
        ] + [pair_sems] * 3 + [core_sems, plane_sems, plane_sems, core_sems, pair_sems] + [pltpu.SemaphoreType.DMA((4, 2, 4))],
        compiler_params=pltpu.CompilerParams(
            collective_id=0, has_side_effects=True, vmem_limit_bytes=60 * 1024 * 1024
        ),
    )(
        field.T,
        quad_weight.reshape(1, 256),
        love_factor.reshape(8, 128),
        pair_table.reshape(1, 8),
        legendre.transpose(1, 0, 2).reshape(8200, 256),
        jnp.asarray(angle_constants()),
    )
    return grid.reshape(256, 256)[:, :LON_COLS].astype(F32)


def solution(mesh):
    placed = (P("lat", "lon"), P("lat"), P("lon", None, "lat"), P(), P("lon"))
    return jax.shard_map(
        per_device, mesh=mesh, in_specs=placed, out_specs=P("lat", "lon"), check_vma=False
    )
```

```python
import math

import jax
import jax.numpy as jnp
import ml_dtypes
import numpy as np
from jax import lax
from jax.experimental import pallas as pl
from jax.experimental.pallas import tpu as pltpu
from jax.sharding import PartitionSpec as P

F32 = jnp.float32
BF16 = jnp.bfloat16
TOTAL_LON = 8640
LON_COLS = 135
DEGREES = 1024
GROUPS = ((0, 4), (1, 7), (2, 6), (3, 5))
FAR_FIRST = (4, 3, 5, 2, 6, 1, 7)


def pair_orders():
    steps = 8 * np.arange(64)
    low = np.concatenate([steps + r for group in GROUPS for r in group])
    high = np.concatenate([steps + 7 - r for group in GROUPS for r in group])
    return low, high


def angle_constants():
    low, high = pair_orders()
    columns = np.arange(LON_COLS)
    made = np.zeros((8, 4, 2, 512, 256), ml_dtypes.bfloat16)
    for group in range(4):
        span = slice(128 * group, 128 * group + 128)
        orders = np.concatenate([low[span], DEGREES - 1 - high[span]])
        sign = np.ones((256, 1))
        if group:
            sign[64:128] = -1.0
            sign[192:256] = -1.0
        for q in range(8):
            turns = orders[:, None] * (LON_COLS * q + columns) % TOTAL_LON
            angle = turns * (2.0 * np.pi / TOTAL_LON)
            both = np.concatenate([np.cos(angle), np.sin(angle) * sign])
            head = both.astype(ml_dtypes.bfloat16)
            made[q, group, 0, :, :LON_COLS] = head
            made[q, group, 1, :, :LON_COLS] = (both - head.astype(np.float64)).astype(ml_dtypes.bfloat16)
    return made


def kernel(
    field_in, quad_in, love_in, pair_in, legendre, angles, out,
    field, quad, love, pair_own, pairs, leg, table, tail, last_rows, s1, r1, rp1, rp2, onehot, rhs, orders_all, s2, r2, s3, r3, four, s4, r4,
    factor, love_rows, spectral, blocks, s6, r6, r7, s8,
    local_sem, sem_pz, sem_pq, sem1, sem2, sem3, sem6, sem7, sem8, sem4,
):
    lon = lax.axis_index("lon")
    x = lax.axis_index("lat")
    z = lon // 8
    q = lon % 8

    def z_device(i):
        return {"lon": i * 8 + q}

    y = q // 2
    core = q % 2

    def zy_device(i, j):
        return {"lon": i * 8 + 2 * j + core}

    other_core = {"lon": z * 8 + 2 * y + 1 - core}

    def q_device(i):
        return {"lon": z * 8 + i}

    def x_device(i):
        return {"lat": i}

    barrier = pltpu.get_barrier_semaphore()
    for d in FAR_FIRST:
        pl.semaphore_signal(barrier, inc=1, device_id=z_device((z + d) % 8))
    for d in FAR_FIRST:
        pl.semaphore_signal(barrier, inc=1, device_id=q_device((q + d) % 8))
    for d in range(1, 4):
        pl.semaphore_signal(barrier, inc=1, device_id=x_device((x + d) % 4))

    field_copy = pltpu.make_async_copy(field_in, field, local_sem.at[2])
    pair_copy = pltpu.make_async_copy(pair_in, pair_own, local_sem.at[3])
    love_copy = pltpu.make_async_copy(love_in, love, local_sem.at[4])
    quad_copy = pltpu.make_async_copy(quad_in, quad, local_sem.at[5])
    leg_copy = pltpu.make_async_copy(legendre, leg, local_sem.at[0])
    table_copy = pltpu.make_async_copy(angles.at[q], table, local_sem.at[1])
    for copy in (pair_copy, field_copy, love_copy, quad_copy, table_copy, leg_copy):
        copy.start()

    unsettled = []

    def send_one(source, target, send_sem, recv_sem, device):
        copy = pltpu.make_async_remote_copy(
            src_ref=source, dst_ref=target, send_sem=send_sem, recv_sem=recv_sem, device_id=device
        )
        copy.start()
        unsettled.append(copy)
        return copy

    def arrived_zy(target, sems, dz, dy):
        pltpu.make_async_remote_copy(
            src_ref=target, dst_ref=target, send_sem=sems.at[0, dz, dy], recv_sem=sems.at[1, dz, dy],
            device_id=zy_device((z + 1) % 8, y),
        ).wait_recv()

    def send(distances, me, size, device, source, target, sems):
        copies = []
        for d in distances:
            to = (me + d) % size
            copy = pltpu.make_async_remote_copy(
                src_ref=source(to, d), dst_ref=target(d),
                send_sem=sems.at[0, d], recv_sem=sems.at[1, d],
                device_id=device(to),
            )
            copy.start()
            copies.append(copy)
        unsettled.extend(copies)
        return copies

    def settle(keep=0):
        while len(unsettled) > keep:
            unsettled.pop(0).wait_send()

    def arrive(copies):
        for copy in copies:
            copy.wait_recv()

    def arrived(target, sems, d):
        pltpu.make_async_remote_copy(
            src_ref=target, dst_ref=target, send_sem=sems.at[0, d], recv_sem=sems.at[1, d],
            device_id=z_device((z + d) % 8),
        ).wait_recv()

    lane = lax.broadcasted_iota(jnp.int32, (1, 128), 1)
    quarter = lane // 32
    step_in_tile = lane // 8

    last_rows[...] = jnp.zeros_like(last_rows)
    pair_copy.wait()
    spread = jnp.concatenate([pair_own[...].astype(F32), jnp.zeros((1, 120), F32)], axis=1)
    for shift in (8, 16, 32, 64):
        spread = spread + pltpu.roll(spread, shift, 1)
    pairs[...] = jnp.broadcast_to(spread, (8, 128))
    field_copy.wait()
    last_rows[0:15, :] = field[120:135, :]
    for h in range(2):
        cols = slice(128 * h, 128 * h + 128)
        runs = [field[40 * c:40 * c + 40, cols] for c in range(3)] + [last_rows[:, cols]]
        for g in range(4):
            packed = pltpu.roll(runs[0], (32 * (0 - g)) % 128, 1) if g else runs[0]
            for c in range(1, 4):
                moved = pltpu.roll(runs[c], (32 * (c - g)) % 128, 1) if c != g else runs[c]
                packed = jnp.where(quarter == c, moved, packed)
            s1[4 * h + g] = packed

    pl.semaphore_wait(barrier, 17)
    copies_pq = send(FAR_FIRST, q, 8, q_device, lambda to, d: pairs, lambda d: rp1.at[q], sem_pq)
    copies1 = send(FAR_FIRST, z, 8, z_device, lambda to, d: s1.at[to], lambda d: r1.at[z], sem1)
    r1[z] = s1[z]
    rp1[q] = pairs[...]

    tile_row = lax.broadcasted_iota(jnp.int32, (8, 128), 0)
    rhs[...] = jnp.zeros_like(rhs)
    s4[...] = jnp.zeros_like(s4)
    tail[...] = jnp.zeros_like(tail)
    love_rows[...] = jnp.zeros_like(love_rows)
    arrive(copies_pq)
    gathered = rp1[0]
    for i in range(1, 8):
        gathered = jnp.where(tile_row == i, rp1[i], gathered)
    rp2[z] = gathered
    send(FAR_FIRST, z, 8, z_device, lambda to, d: rp2.at[z], lambda d: rp2.at[z], sem_pz)

    pair_lane = pairs[0:1, :]
    love_copy.wait()
    love_rows[1:9, :] = love[...]
    love16 = love_rows[...]
    lane_row = lax.broadcasted_iota(jnp.int32, (128, 128), 0).astype(F32)
    step_f = step_in_tile.astype(F32)

    def shifted_love(start):
        whole = jnp.floor(start * (1.0 / 128.0))
        picked = jnp.where(lane_row == start - 128.0 * whole, 1.0, 0.0).astype(F32)
        rows = jnp.dot(love16, picked, preferred_element_type=F32, precision=lax.Precision.HIGHEST)
        for bit in (4, 2, 1):
            half = jnp.floor(whole * (1.0 / bit))
            odd = half - 2.0 * jnp.floor(half * 0.5)
            rows = jnp.where(odd > 0.5, pltpu.roll(rows, 16 - bit, 0), rows)
        return rows

    def column_ids(t0):
        return 128 * tile_row + (16 * t0 + step_in_tile)

    pair_int = pair_lane.astype(jnp.int32)
    for t0 in range(8):
        low_love = shifted_love(step_f + (pair_lane + (16.0 * t0 + 128.0)))
        high_love = shifted_love(step_f + (16.0 * t0 + 127.0))
        is_low = column_ids(t0) < DEGREES - pair_int
        factor[pl.ds(t0, 8, stride=8), :] = jnp.where(is_low, low_love[0:8], high_love[0:8])
        if t0 == 0:
            factor[64:72, :] = high_love[8:16]

    place = lax.broadcasted_iota(jnp.int32, (1, 1024), 1)
    group = place % 512 // 128
    other = jnp.where(group == 0, 4, 8 - group)
    residue = jnp.where(place % 128 < 64, group, other)
    wanted = (8 * (place % 64) + jnp.where(place < 512, residue, 7 - residue)).astype(F32)
    diagonal = lax.broadcasted_iota(jnp.int32, (16, 128), 0) % 8 == lane

    table_copy.wait()
    arrive(copies1)
    f = [r1[i] for i in range(8)]
    a = [f[i] - f[i + 4] for i in range(4)]
    b = [f[i] + f[i + 4] for i in range(4)]
    root = math.sqrt(0.5)
    a13m = root * (a[1] - a[3])
    a13p = root * (a[1] + a[3])
    parts = (
        (b[0] + b[1] + b[2] + b[3], b[0] - b[1] + b[2] - b[3]),
        (a[0] + a13m, -a[2] - a13p),
        (b[0] - b[2], b[3] - b[1]),
        (a[0] - a13m, a[2] - a13p),
    )

    def turned(value, by):
        return pltpu.roll(value, by % 128, value.ndim - 1) if by % 128 else value

    for g in range(4):
        re, im = parts[g]
        for c in range(4):
            rhs[g, 40 * c:40 * c + 40, :] = jnp.where(
                quarter < 2,
                jnp.where(quarter == 0, turned(re, -32 * c), turned(im, 32 - 32 * c)),
                jnp.where(quarter == 2, turned(re, 64 - 32 * c), turned(im, 96 - 32 * c)),
            )
    for g in range(4):
        value = rhs[g]
        head = value.astype(BF16).astype(F32)
        both = jnp.where(lane < 64, head, value - head).astype(BF16)
        first = jnp.dot(table[g, 0], both, preferred_element_type=F32)
        second = jnp.dot(table[g, 1], both, preferred_element_type=F32)
        total = first + turned(first, 64) + second
        d1, d2 = total[0:256], total[256:512]
        if g:
            spectrum = d1 + jnp.where(quarter == 0, turned(d2, 96), -turned(d2, 32))
            flipped = jnp.where(quarter == 1, -spectrum, spectrum)
            rows = (spectrum[0:64], flipped[64:128], spectrum[128:192], flipped[192:256])
        else:
            plain = jnp.where(quarter == 0, d1, -turned(d2, 32))
            other = jnp.where(quarter == 0, turned(d1, 96), -d2)
            rows = (plain[0:64], other[64:128], plain[128:192], other[192:256])
        for half in range(2):
            at = 128 * g + 64 * half
            for o in range(2):
                value = rows[2 * o + half]
                head = value.astype(BF16).astype(F32)
                orders_all[o, at:at + 64, :] = jnp.where(lane < 64, head, turned(value - head, 64)).astype(BF16)

    odd = z % 2
    near_other = 2 + 4 * odd
    far_other = 6 - 4 * odd

    def plane_pair(half, i):
        return (z // 2 + odd + 3 + 2 * half + i) % 4

    copies2 = []
    for half in range(2):
        for d in ((1, 7, near_other), (3, 4, 5, far_other))[half]:
            arrived(rp2.at[z], sem_pz, d)
        columns = []
        for i in range(2):
            first, second = rp2[2 * plane_pair(half, i)], rp2[2 * plane_pair(half, i) + 1]
            for to in range(8):
                both = jnp.concatenate([
                    jnp.broadcast_to(first[to:to + 1], (8, 128)), jnp.broadcast_to(second[to:to + 1], (8, 128))
                ], axis=0)
                columns.append(jnp.sum(jnp.where(diagonal, both, 0.0), axis=1, keepdims=True))
        for i in range(2):
            for to in range(8):
                at = pl.multiple_of(64 * to + 16 * plane_pair(half, i), 16)
                onehot[pl.ds(at, 16), :] = jnp.where(columns[8 * i + to] == wanted, 1.0, 0.0).astype(BF16)
        rows = jnp.concatenate([
            onehot[pl.ds(pl.multiple_of(
                64 * (2 * ((y + dy) % 4) + (core + e) % 2) + 16 * plane_pair(half, i), 16
            ), 16), :]
            for e in range(2) for dy in range(4) for i in range(2)
        ], axis=0)
        low_part = jnp.dot(rows[:, 0:512], orders_all[0], preferred_element_type=F32)
        high_part = jnp.dot(rows[:, 512:1024], orders_all[1], preferred_element_type=F32)
        in_slots = jnp.where(lane < 64, low_part + turned(low_part, 64), high_part + turned(high_part, 64))
        s2[half] = in_slots.reshape(2, 128, 128)
        copies2.append(send_one(
            s2.at[half, 1], r2.at[half], sem2.at[0, half], sem2.at[1, half], other_core
        ))
    settle(2)

    for half in range(2):
        copies2[half].wait_recv()
        total = s2[half, 0] + r2[half]
        for dy in range(4):
            for i in range(2):
                for plane in range(2):
                    at = 32 * dy + 16 * i + 8 * plane
                    s3[dy, 2 * plane_pair(half, i) + plane] = total[at:at + 8]
        for dz in ((far_other, 1, 7, 0), (4, 3, 5, near_other))[half]:
            for dy in (2, 1, 3, 0):
                if isinstance(dz, int) and dz == 0 and dy == 0:
                    continue
                send_one(
                    s3.at[dy, (z + dz) % 8], r3.at[y, z], sem3.at[0, dz, dy], sem3.at[1, dz, dy],
                    zy_device((z + dz) % 8, (y + dy) % 4),
                )
    r3[y, z] = s3[0, z]

    quad_copy.wait()
    leg_copy.wait()
    tail[0:8, :] = leg[8192:8200, :].astype(F32)
    settle(31)
    for dz in range(8):
        for dy in range(4):
            if dz or dy:
                arrived_zy(r3.at[y, z], sem3, dz, dy)
    own_sums = [r3[0, i] + r3[1, i] + r3[2, i] + r3[3, i] for i in range(8)]
    for r in range(2):
        for o in range(2):
            j = 2 * o + r
            for h in range(2):
                cols = slice(128 * h, 128 * h + 128)
                tile = turned(own_sums[4 * h], -32 * j)
                for g in range(1, 4):
                    tile = jnp.where(quarter == g, turned(own_sums[4 * h + g], 32 * (g - j)), tile)
                at = 16 * r + 8 * o
                four[at:at + 8, cols] = tile / float(TOTAL_LON) * quad[0:1, cols]
    fourier = four[...].astype(BF16)

    own_slot = lane % 8 == tile_row
    low_limit = DEGREES - pair_int - step_in_tile
    tail_rows = tail[...].astype(BF16)

    def analysed(piece, is_low, r):
        if is_low is None:
            picked = piece[16 * r + 8:16 * r + 16]
        else:
            picked = jnp.where(is_low, piece[16 * r:16 * r + 8], piece[16 * r + 8:16 * r + 16])
        return jnp.sum(jnp.where(own_slot, picked, 0.0), axis=0, keepdims=True)

    product = lax.dot_general(fourier, tail_rows, (((1,), (1,)), ((), ())), preferred_element_type=F32)
    for r in range(2):
        s4[0, 32 + r:33 + r, :] = analysed(product, None, r)
    copies4 = []
    for chunk in range(4):
        product = lax.dot_general(
            fourier, leg[2048 * chunk:2048 * chunk + 2048, :], (((1,), (1,)), ((), ())), preferred_element_type=F32
        )
        for row in range(16):
            is_low = jnp.broadcast_to(16 * (16 * chunk + row) < low_limit, (8, 128))
            for r in range(2):
                s4[chunk, 16 * r + row:16 * r + row + 1, :] = analysed(
                    product[:, 128 * row:128 * row + 128], is_low, r
                )
        size = 32 if chunk else 40
        copies4.append(send(
            (2, 1, 3), x, 4, x_device,
            lambda to, d: s4.at[chunk, pl.ds(0, size)], lambda d: r4.at[d, chunk, pl.ds(0, size)], sem4.at[chunk],
        ))

    settle(12)
    profile = jnp.zeros((32, 256), F32)
    for chunk in range(4):
        arrive(copies4[chunk])
        total = s4[chunk] + r4[1, chunk] + r4[2, chunk] + r4[3, chunk]
        scale = factor[16 * chunk:16 * chunk + 16, :]
        spectral[chunk] = jnp.concatenate([total[0:16] * scale, total[16:32] * scale], axis=0).astype(BF16).astype(F32)
        for row in range(16):
            is_low = jnp.broadcast_to(16 * (16 * chunk + row) < low_limit, (8, 128))
            pieces = []
            for r in range(2):
                line = jnp.broadcast_to(spectral[chunk, 16 * r + row:16 * r + row + 1, :], (8, 128))
                line = jnp.where(own_slot, line, 0.0)
                pieces += [jnp.where(is_low, line, 0.0), jnp.where(is_low, 0.0, line)]
            blocks[chunk, :, 128 * row:128 * row + 128] = jnp.concatenate(pieces, axis=0).astype(BF16)
        profile = profile + jnp.dot(
            blocks[chunk], leg[2048 * chunk:2048 * chunk + 2048, :], preferred_element_type=F32
        )
        if chunk == 0:
            last = (total[32:40] * factor[64:65, :]).astype(BF16).astype(F32)
            pieces = []
            for r in range(2):
                line = jnp.where(own_slot, jnp.broadcast_to(last[r:r + 1], (8, 128)), 0.0)
                pieces += [jnp.zeros((8, 128), F32), line]
            profile = profile + jnp.dot(
                jnp.concatenate(pieces, axis=0).astype(BF16), tail_rows, preferred_element_type=F32
            )
    profile = profile.astype(BF16).astype(F32)

    for h in range(2):
        for g in range(4):
            tile = turned(profile[0:8, 128 * h:128 * h + 128], -32 * g)
            for j in range(1, 4):
                at = 16 * (j % 2) + 8 * (j // 2)
                tile = jnp.where(
                    quarter == j, turned(profile[at:at + 8, 128 * h:128 * h + 128], 32 * (j - g)), tile
                )
            s6[4 * h + g] = tile
    for dz in FAR_FIRST + (0,):
        for dy in (2, 1, 3, 0):
            if dz or dy:
                send_one(
                    s6.at[(z + dz) % 8], r6.at[y, z], sem6.at[0, dz, dy], sem6.at[1, dz, dy],
                    zy_device((z + dz) % 8, (y + dy) % 4),
                )
    r6[y, z] = s6[z]
    settle(31)

    copies7 = []
    for dy in (0, 1, 3, 2):
        for dz in range(8):
            if dz or dy:
                arrived_zy(r6.at[y, z], sem6, dz, dy)
        row = (y - dy + 4) % 4
        r7[row, core] = r6[row].reshape(64, 128).astype(BF16)
        copies7.append(send_one(
            r7.at[row, core], r7.at[row, core], sem7.at[0, dy], sem7.at[1, dy], other_core
        ))
    settle(4)
    natural = jnp.zeros((128, 1024), F32)
    for e in range(2):
        if e:
            arrive(copies7)
        part = (core + e) % 2
        left = jnp.concatenate([r7[row, part] for row in range(4)], axis=0)
        right = jnp.concatenate(
            [onehot[pl.ds(pl.multiple_of(128 * row + 64 * part, 64), 64), :] for row in range(4)], axis=0
        )
        natural = natural + lax.dot_general(left, right, (((0,), (0,)), ((), ())), preferred_element_type=F32)
    wide_lane = lax.broadcasted_iota(jnp.int32, (1, 256), 1)
    second_half = wide_lane % 128 >= 64
    waves = []
    for g in range(4):
        low = slice(128 * g, 128 * g + 128)
        high = slice(512 + 128 * g, 640 + 128 * g)
        re = jnp.concatenate([natural[0:32, low], natural[64:96, high]], axis=1)
        im = jnp.concatenate([natural[32:64, low], natural[96:128, high]], axis=1)
        if g:
            left = jnp.concatenate([re, jnp.where(second_half, -im, im)], axis=0)
        else:
            re = jnp.where(wide_lane == 0, 0.5 * re, re)
            im = jnp.where(wide_lane == 0, 0.5 * im, im)
            left = jnp.concatenate([
                jnp.where(second_half, 0.0, re), jnp.where(second_half, 0.0, im),
                jnp.where(second_half, re, 0.0), jnp.where(second_half, im, 0.0),
            ], axis=0)
        left = left.astype(BF16)
        by_cos = jnp.dot(left, table[g, 0, 0:256], preferred_element_type=F32) + jnp.dot(
            left, table[g, 1, 0:256], preferred_element_type=F32
        )
        by_sin = jnp.dot(left, table[g, 0, 256:512], preferred_element_type=F32) + jnp.dot(
            left, table[g, 1, 256:512], preferred_element_type=F32
        )
        if g:
            waves.append((by_cos[0:32] - by_sin[32:64], by_sin[0:32] + by_cos[32:64]))
        else:
            waves.append((by_cos[0:32] - by_sin[32:64], by_cos[64:96] - by_sin[96:128]))
    (w0, w4), (re1, im1), (re2, im2), (re3, im3) = waves
    even0, even1 = w0 + w4, w0 - w4
    re_sum, re_dif = re1 + re3, root * (re1 - re3)
    im_dif, im_sum = im1 - im3, root * (im1 + im3)
    b0, b1, b2, b3 = even0 + re2, even1 - im2, even0 - re2, even1 + im2
    a0, a1, a2, a3 = re_sum, re_dif - im_sum, -im_dif, -re_dif - im_sum
    for i, value in enumerate((b0 + a0, b1 + a1, b2 + a2, b3 + a3, b0 - a0, b1 - a1, b2 - a2, b3 - a3)):
        s8[i] = (2.0 * value).astype(BF16)

    copies8 = send(FAR_FIRST, z, 8, z_device, lambda to, d: s8.at[to], lambda d: out.at[z], sem8)
    own_copy = pltpu.make_async_copy(s8.at[z], out.at[z], local_sem.at[6])
    own_copy.start()
    settle(7)
    arrive(copies8)
    own_copy.wait()
    settle()


def per_device(field, quad_weight, legendre, love_factor, pair_table):
    anywhere = pl.BlockSpec(memory_space=pl.ANY)
    pair_sems = pltpu.SemaphoreType.DMA((2, 8))
    plane_sems = pltpu.SemaphoreType.DMA((2, 8, 4))
    core_sems = pltpu.SemaphoreType.DMA((2, 4))
    grid = pl.pallas_call(
        kernel,
        out_shape=jax.ShapeDtypeStruct((8, 32, 256), BF16),
        in_specs=[anywhere] * 6,
        out_specs=anywhere,
        scratch_shapes=[
            pltpu.VMEM((LON_COLS, 256), F32),
            pltpu.VMEM((1, 256), F32),
            pltpu.VMEM((8, 128), F32),
            pltpu.VMEM((1, 8), jnp.int32),
            pltpu.VMEM((8, 128), F32),
            pltpu.VMEM((8200, 256), BF16),
            pltpu.VMEM((4, 2, 512, 256), BF16),
            pltpu.VMEM((128, 256), F32),
            pltpu.VMEM((40, 256), F32),
            pltpu.VMEM((8, 40, 128), F32),
            pltpu.VMEM((8, 40, 128), F32),
            pltpu.VMEM((8, 8, 128), F32),
            pltpu.VMEM((8, 8, 128), F32),
            pltpu.VMEM((512, 1024), BF16),
            pltpu.VMEM((4, 256, 128), F32),
            pltpu.VMEM((2, 512, 128), BF16),
            pltpu.VMEM((2, 2, 128, 128), F32),
            pltpu.VMEM((2, 128, 128), F32),
            pltpu.VMEM((4, 8, 8, 128), F32),
            pltpu.VMEM((4, 8, 8, 128), F32),
            pltpu.VMEM((32, 256), F32),
            pltpu.VMEM((4, 40, 128), F32),
            pltpu.VMEM((4, 4, 40, 128), F32),
            pltpu.VMEM((72, 128), F32),
            pltpu.VMEM((16, 128), F32),
            pltpu.VMEM((4, 32, 128), F32),
            pltpu.VMEM((4, 32, 2048), BF16),
            pltpu.VMEM((8, 8, 128), F32),
            pltpu.VMEM((4, 8, 8, 128), F32),
            pltpu.VMEM((4, 2, 64, 128), BF16),
            pltpu.VMEM((8, 32, 256), BF16),
            pltpu.SemaphoreType.DMA((7,)),
        ] + [pair_sems] * 3 + [core_sems, plane_sems, plane_sems, core_sems, pair_sems] + [pltpu.SemaphoreType.DMA((4, 2, 4))],
        compiler_params=pltpu.CompilerParams(
            collective_id=0, has_side_effects=True, vmem_limit_bytes=60 * 1024 * 1024
        ),
    )(
        field.T,
        quad_weight.reshape(1, 256),
        love_factor.reshape(8, 128),
        pair_table.reshape(1, 8),
        legendre.transpose(1, 0, 2).reshape(8200, 256),
        jnp.asarray(angle_constants()),
    )
    return grid.reshape(256, 256)[:, :LON_COLS].astype(F32)


def solution(mesh):
    placed = (P("lat", "lon"), P("lat"), P("lon", None, "lat"), P(), P("lon"))
    return jax.shard_map(
        per_device, mesh=mesh, in_specs=placed, out_specs=P("lat", "lon"), check_vma=False
    )
```
